768 devices in a mesh: dp: 96 (over x, z, core), tensor: 8 (over y).
Axes of the slice: x: 4, y: 8, z: 12, core: 2. Of those that a mesh axis runs over, the one named last changes fastest.
Arguments:
- tokens: bfloat16 [12288, 3584], P('dp', 'tensor'), may hold values from -6 to 6
- cotangent: bfloat16 [12288, 3584], P('dp', 'tensor'), may hold values from -6 to 6
- expert_ids: int32 [12288, 2], P('dp'), may hold values from 0 to 95, all different within a row; in each aligned block of 128 rows (0 to 127, 128 to 255, ...) at most 3 rows name the same one
- route_probs: float32 [12288, 2], P('dp'), may hold values from 0.05 to 1
- up_weight: bfloat16 [96, 3584, 2432], P('dp', 'tensor'), may hold values from -0.09375 to 0.09375
- down_weight: bfloat16 [96, 2432, 3584], P('dp', None, 'tensor'), may hold values from -0.125 to 0.125
Outputs:
- mixed: bfloat16 [12288, 3584], P('dp', 'tensor')
- input_grad: bfloat16 [12288, 3584], P('dp', 'tensor')
- prob_grad: float32 [12288, 2], P('dp')
The draws below stay inside these ranges and needn't reach their ends.
Inputs may be any that keep to these rules, and one draw needn't show every extreme that they name: `expert_ids`: each row names two different experts. Among the rows of one index of dp (aligned blocks of 128 rows), no expert is named more than 3 times, a bound that some block reaches.
All inputs are finite; a program needn't handle non-finite values.
Results may differ from the reference program's by a relative error of at most 0.024.
Values may be sent and summed in bfloat16 or wider, within the bound.
No kernel may reach another device: no remote copies, remote signals or barrier semaphores. Data moves between devices by JAX's collectives and lax.ppermute only.
A program may use at most 64 MiB of HBM per device.

```python
import math
import jax
import jax.numpy as jnp
import numpy as np
from jax import lax

D = 3584
F = 2432
TOK_DEV = 128
EXPERTS = 96
CAP = 3
TOKENS = 12288
N_DP = 96
N_TENSOR = 8


def block_levels(rng, extent, shards, least, top_value):
    def one(position, shards_of):
        steps = jax.random.uniform(jax.random.fold_in(jax.random.fold_in(rng, 6), position), (shards_of,), jnp.float32, least / len(shards), top_value / len(shards))
        return jnp.repeat(jnp.exp(steps), extent[position] // shards_of).reshape((-1,) + (1,) * (len(extent) - position - 1))

    loudness = one(*shards[0])
    for cut in shards[1:]:
        loudness = loudness * one(*cut)
    return loudness


def assign_block(key, own, number, rows, number_of, top, most, slope):
    sequence = jax.random.permutation(key, number_of)
    crowded, ordinary = load_shares(number_of, rows * top, most, slope, True), load_shares(number_of, rows * top, most, slope, False)
    places = jnp.arange(number_of)

    def named(lengths, turn):
        used = int((lengths > 0).sum())
        fixed = max(1, used // 4)
        passed = fixed + (places - fixed + turn * (used - fixed)) % max(1, number_of - fixed)
        return jnp.zeros((number_of,), jnp.int32).at[sequence[jnp.where(places < fixed, places, passed)]].set(jnp.asarray(lengths, jnp.int32))

    lengths = jnp.where(number % 4 == 0, named(crowded, number // 4), named(ordinary, number - number // 4 - 1))
    mixed = jax.random.permutation(jax.random.fold_in(own, 3), number_of)
    source_of, taker = mixed[0:number_of // 2 * 2:2], mixed[1:number_of // 2 * 2:2]
    margin = jnp.minimum(lengths[source_of] - 1, most - lengths[taker]) // 2
    margin = jnp.where((source_of == sequence[0]) | (taker == sequence[0]) | (lengths[taker] == 0), 0, jnp.maximum(margin, 0))
    passed = jax.random.randint(jax.random.fold_in(own, 4), (number_of // 2,), 0, 1 << 20) % (margin + 1)
    lengths = lengths.at[source_of].add(-passed).at[taker].add(passed)
    members = jnp.searchsorted(jnp.cumsum(lengths), jnp.arange(rows * top), side="right").astype(jnp.int32)
    table = members.reshape(top, rows).T
    table = table[jax.random.permutation(jax.random.fold_in(own, 1), rows)]
    turn = jax.random.randint(jax.random.fold_in(own, 2), (rows, 1), 0, top)
    return jnp.take_along_axis(table, (jnp.arange(top)[None, :] + turn) % top, axis=1)


def load_shares(count, total, reach, lean, full):
    loads = [(1 << 20) // math.isqrt(grade ** lean) + 1 for grade in range(1, count + 1)]
    largest = reach if full else min(reach, max(-(-total // count), total * loads[0] // sum(loads)))
    least = 1 if total - largest >= count - 1 else 0
    given, surplus = [largest] + [least] * (count - 1), total - largest - least * (count - 1)
    while surplus > 0:
        movable = [i for i in range(1, count) if given[i] < largest] or [i for i in range(1, count) if given[i] < reach]
        whole, budget = sum([loads[i] for i in movable]), surplus
        for i in movable:
            extra = min(reach - given[i], max(1, budget * loads[i] // whole), surplus)
            given[i] = given[i] + extra
            surplus = surplus - extra
    return np.array(given)


def gaussian(rng, dims, deviation, bound, cuts=(), kind=jnp.bfloat16):
    array = deviation * jax.random.normal(rng, dims, jnp.float32)
    if cuts:
        array = array * block_levels(rng, dims, cuts, -0.22, 0.18)
    return jnp.clip(array, -bound, bound).astype(kind)


def setup_inputs(seed: int = 0) -> dict:
    streams_of = jax.random.split(jax.random.key(seed), 7)
    tokens = gaussian(streams_of[0], (TOKENS, D), 1.0, 6.0, ((0, 96), (1, 8)))
    cotangent = gaussian(streams_of[1], (TOKENS, D), 1.0, 6.0, ((0, 96), (1, 8)))
    expert_ids_keys = jax.random.split(jax.random.fold_in(streams_of[2], 1), TOKENS // TOK_DEV)
    expert_ids_turns = jax.random.permutation(jax.random.fold_in(streams_of[2], 3), TOKENS // TOK_DEV)
    expert_ids = jax.vmap(lambda own, number: assign_block(jax.random.fold_in(streams_of[2], 2), own, number, TOK_DEV, EXPERTS, 2, CAP, 2))(expert_ids_keys, expert_ids_turns).reshape((TOKENS, 2))
    route_probs = jnp.clip(jnp.exp(math.log(1.0) - 2.9957323 * jax.random.uniform(streams_of[3], (TOKENS, 2), jnp.float32) ** block_levels(streams_of[3], (TOKENS, 2), ((0, 96),), -0.2, 0.2)), 0.05, 1.0)
    up_weight = gaussian(streams_of[4], (EXPERTS, D, F), D ** -0.5, 0.09375, ((0, 96), (1, 8)))
    down_weight = gaussian(streams_of[5], (EXPERTS, F, D), F ** -0.5, 0.125, ((0, 96), (2, 8)))
    return {"tokens": tokens, "cotangent": cotangent, "expert_ids": expert_ids, "route_probs": route_probs, "up_weight": up_weight, "down_weight": down_weight}


def slot_ranks(route_ids, blocks, rows_each, expert_count):
    grouped = route_ids.reshape(blocks, rows_each * 2)
    onehot = (grouped[:, :, None] == jnp.arange(expert_count, dtype=jnp.int32)[None, None, :]).astype(jnp.int32)
    rank_table = jnp.cumsum(onehot, axis=1) - 1
    return jnp.sum(onehot * rank_table, axis=2).reshape(blocks * rows_each, 2).astype(jnp.int32)


def rounded_sum(parts):
    rounded = lax.optimization_barrier(parts.astype(jnp.bfloat16))
    return jnp.sum(rounded.astype(jnp.float32), axis=0)


def reference(tokens, cotangent, expert_ids, route_probs, up_weight, down_weight):
    feat_local = D // N_TENSOR
    slot_index = slot_ranks(expert_ids, N_DP, TOK_DEV, EXPERTS)
    source = (jnp.arange(TOKENS, dtype=jnp.int32) // TOK_DEV)[:, None]
    flat_slot = ((expert_ids * N_DP + source) * CAP + slot_index).astype(jnp.int32)
    slot_total = EXPERTS * N_DP * CAP
    token_index = jnp.broadcast_to(jnp.arange(TOKENS, dtype=jnp.int32)[:, None], (TOKENS, 2))
    row_table = jnp.full((slot_total,), TOKENS, jnp.int32).at[flat_slot.reshape(-1)].set(token_index.reshape(-1))
    prob_table = jnp.zeros((slot_total,), jnp.float32).at[flat_slot.reshape(-1)].set(route_probs.reshape(-1))
    padded_tokens = jnp.concatenate([tokens, jnp.zeros((1, D), tokens.dtype)], 0)
    padded_cot = jnp.concatenate([cotangent, jnp.zeros((1, D), cotangent.dtype)], 0)

    def one_expert(packed):
        row_index, row_prob, up_full, down_full = packed
        row_block = padded_tokens[row_index]
        grad_block = (row_prob[:, None] * padded_cot[row_index].astype(jnp.float32)).astype(jnp.bfloat16)
        pieces = row_block.astype(jnp.float32).reshape(-1, N_TENSOR, feat_local)
        up_parts = jnp.einsum("rnd,ndf->nrf", pieces, up_full.astype(jnp.float32).reshape(N_TENSOR, feat_local, F))
        up_sum = rounded_sum(up_parts)
        hidden = jax.nn.silu(up_sum).astype(jnp.bfloat16)
        expert_out = jnp.dot(hidden, down_full, preferred_element_type=jnp.float32).astype(jnp.bfloat16)
        grad_pieces = grad_block.astype(jnp.float32).reshape(-1, N_TENSOR, feat_local)
        hidden_parts = jnp.einsum("rnd,fnd->nrf", grad_pieces, down_full.astype(jnp.float32).reshape(F, N_TENSOR, feat_local))
        hidden_grad = rounded_sum(hidden_parts)
        up_sigmoid = jax.nn.sigmoid(up_sum)
        up_grad = (hidden_grad * up_sigmoid * (1.0 + up_sum * (1.0 - up_sigmoid))).astype(jnp.bfloat16)
        input_part = jnp.dot(up_grad, up_full.T, preferred_element_type=jnp.float32).astype(jnp.bfloat16)
        return expert_out, input_part

    expert_out, input_part = lax.map(one_expert, (row_table.reshape(EXPERTS, N_DP * CAP), prob_table.reshape(EXPERTS, N_DP * CAP), up_weight, down_weight))
    out_flat = expert_out.reshape(slot_total, D)
    part_flat = input_part.reshape(slot_total, D)
    first = out_flat[flat_slot[:, 0]].astype(jnp.float32)
    second = out_flat[flat_slot[:, 1]].astype(jnp.float32)
    mixed = (route_probs[:, 0:1] * first + route_probs[:, 1:2] * second).astype(jnp.bfloat16)
    input_grad = (part_flat[flat_slot[:, 0]].astype(jnp.float32) + part_flat[flat_slot[:, 1]].astype(jnp.float32)).astype(jnp.bfloat16)
    cot_float = cotangent.astype(jnp.float32)
    prob_grad = jnp.stack([jnp.sum(cot_float * first, axis=1), jnp.sum(cot_float * second, axis=1)], axis=1)
    return mixed, input_grad, prob_grad
```

```python
import jax
import jax.numpy as jnp
from jax import lax
from jax.experimental import pallas as pl
from jax.experimental.pallas import tpu as pltpu
from jax.sharding import PartitionSpec as P

CAP = 3
LANES = 128
BLOCK = 24
ROWS = 320
F32 = jnp.float32
BF16 = jnp.bfloat16
MIB = 1024 * 1024


def params(mib):
    return pltpu.CompilerParams(vmem_limit_bytes=mib * MIB)


def one_hots(ids_ref, experts):
    tokens = ids_ref.shape[1]
    expert = lax.broadcasted_iota(jnp.int32, (experts, tokens), 0)
    named = [(ids_ref[k : k + 1, :] == expert).astype(F32) for k in range(2)]
    before = lax.broadcasted_iota(jnp.int32, (tokens, tokens), 0)
    after = lax.broadcasted_iota(jnp.int32, (tokens, tokens), 1)
    earlier = (before < after).astype(F32).astype(BF16)
    slot = jnp.dot((named[0] + named[1]).astype(BF16), earlier, preferred_element_type=F32)
    return named, slot


def tile_of(first, second, j):
    if j < 3:
        return first[:, j * LANES : (j + 1) * LANES]
    if j < 6:
        return second[:, (j - 3) * LANES : (j - 2) * LANES]
    return jnp.concatenate([first[:, 3 * LANES :], second[:, 3 * LANES :]], axis=1)


def pair_of(tiles):
    half = LANES // 2
    first = jnp.concatenate(tiles[0:3] + [tiles[6][:, :half]], axis=1)
    second = jnp.concatenate(tiles[3:6] + [tiles[6][:, half:]], axis=1)
    return first, second


def dispatch_kernel(ids_ref, probs_ref, tok_ref, cot_ref, out_ref, scratch):
    experts = out_ref.shape[0] // BLOCK
    named, slot = one_hots(ids_ref, experts)
    either = named[0] + named[1]
    weight = named[0] * probs_ref[0:1, :] + named[1] * probs_ref[1:2, :]
    across = (((1,), (1,)), ((), ()))
    for s in range(CAP):
        here = (slot == s).astype(F32)
        pick = (either * here).astype(BF16)
        rows = lax.dot_general(pick, tok_ref[...], across, preferred_element_type=F32)
        grads = lax.dot_general(pick, cot_ref[...], across, preferred_element_type=F32)
        grads = grads * jnp.sum(weight * here, axis=1, keepdims=True)
        for j in range(7):
            scratch[pl.ds(s * 7 + j, experts, stride=BLOCK), :] = tile_of(rows, grads, j)
    for r in range(7 * CAP, BLOCK):
        scratch[pl.ds(r, experts, stride=BLOCK), :] = jnp.zeros((experts, LANES), F32)
    out_ref[...] = scratch[...].astype(BF16)


def up_kernel(block_ref, up_ref, down_ref, out_ref, scratch):
    sources = block_ref.shape[0] // BLOCK
    hidden = up_ref.shape[1]
    scratch[...] = block_ref[...].astype(F32)
    rows, grads = [], []
    for s in range(CAP):
        tiles = [scratch[pl.ds(s * 7 + j, sources, stride=BLOCK), :] for j in range(7)]
        first, second = pair_of(tiles)
        rows.append(first)
        grads.append(second)
    pad = jnp.zeros((ROWS - CAP * sources, up_ref.shape[0]), F32)
    rows = jnp.concatenate(rows + [pad], axis=0).astype(BF16)
    grads = jnp.concatenate(grads + [pad], axis=0).astype(BF16)
    for left, weight, base in ((rows, up_ref, 0), (grads, down_ref, hidden)):
        for at in range(0, hidden, 512):
            to = min(at + 512, hidden)
            out_ref[:, base + at : base + to] = jnp.dot(
                left, weight[:, at:to], preferred_element_type=F32
            ).astype(BF16)


def middle_kernel(sum_ref, out_ref):
    hidden = sum_ref.shape[1] // 2
    up_sum = sum_ref[:, :hidden].astype(F32)
    grad = sum_ref[:, hidden:].astype(F32)
    sigmoid = 1.0 / (1.0 + jnp.exp(-up_sum))
    act = (up_sum * sigmoid).astype(BF16)
    out_ref[:, :hidden] = act
    out_ref[:, hidden : 2 * hidden] = (
        grad * sigmoid * (1.0 + up_sum * (1.0 - sigmoid))
    ).astype(BF16)
    score = jnp.sum(act.astype(F32) * grad, axis=1, keepdims=True)
    high = score.astype(BF16).astype(F32)
    lane = lax.broadcasted_iota(jnp.int32, (sum_ref.shape[0], LANES), 1)
    out_ref[:, 2 * hidden :] = jnp.where(
        lane == 0, high, jnp.where(lane == 1, score - high, 0.0)
    ).astype(BF16)


def down_kernel(join_ref, up_ref, down_ref, out_ref, scratch):
    sources = out_ref.shape[0] // BLOCK
    hidden = up_ref.shape[1]
    across = (((1,), (1,)), ((), ()))
    out = lax.dot_general(
        join_ref[:, :hidden], down_ref[...], across, preferred_element_type=F32
    )
    part = lax.dot_general(
        join_ref[:, hidden : 2 * hidden], up_ref[...], across, preferred_element_type=F32
    )
    score = join_ref[:, 2 * hidden :].astype(F32)
    for s in range(CAP):
        rows = slice(s * sources, (s + 1) * sources)
        for j in range(7):
            scratch[pl.ds(s * 7 + j, sources, stride=BLOCK), :] = tile_of(out[rows], part[rows], j)
        scratch[pl.ds(7 * CAP + s, sources, stride=BLOCK), :] = score[rows]
    out_ref[...] = scratch[...].astype(BF16)


def combine_kernel(ids_ref, probs_ref, block_ref, mixed_ref, grad_ref, score_ref, scratch):
    experts = block_ref.shape[0] // BLOCK
    named, slot = one_hots(ids_ref, experts)
    scratch[...] = block_ref[...].astype(F32)
    along = (((0,), (0,)), ((), ()))
    outs, parts, picks = [], [], []
    scores = [jnp.zeros((1, ids_ref.shape[1]), F32) for _ in range(2)]
    for s in range(CAP):
        here = (slot == s).astype(F32)
        tiles = [scratch[pl.ds(s * 7 + j, experts, stride=BLOCK), :] for j in range(7)]
        first, second = pair_of(tiles)
        outs.append(first)
        parts.append(second)
        picks.append(jnp.concatenate([named[0] * here, named[1] * here], axis=1))
        tail = scratch[pl.ds(7 * CAP + s, experts, stride=BLOCK), :]
        value = tail[:, 0:1] + tail[:, 1:2]
        for k in range(2):
            scores[k] += jnp.sum(named[k] * here * value, axis=0, keepdims=True)
    outs = jnp.concatenate(outs, axis=0).astype(BF16)
    parts = jnp.concatenate(parts, axis=0).astype(BF16)
    picks = jnp.concatenate(picks, axis=0)
    tokens = ids_ref.shape[1]
    either = (picks[:, :tokens] + picks[:, tokens:]).astype(BF16)
    got = lax.dot_general(outs, picks.astype(BF16), along, preferred_element_type=F32)
    mixed_ref[...] = (
        got[:, :tokens] * probs_ref[0:1, :] + got[:, tokens:] * probs_ref[1:2, :]
    ).astype(BF16)
    grad_ref[...] = lax.dot_general(parts, either, along, preferred_element_type=F32).astype(BF16)
    score_ref[...] = jnp.concatenate(scores, axis=0) / probs_ref[...]


def exchange(block, experts):
    block = block.reshape(experts, BLOCK, LANES)
    block = lax.all_to_all(block, "dp", split_axis=0, concat_axis=0, tiled=True)
    return block.reshape(experts * BLOCK, LANES)


def per_device(tokens, cotangent, expert_ids, route_probs, up_weight, down_weight):
    count, feat = tokens.shape
    experts = lax.axis_size("dp")
    hidden = up_weight.shape[2]
    ids, probs = expert_ids.T, route_probs.T
    up, down = up_weight[0], down_weight[0].T
    packed = jax.ShapeDtypeStruct((experts * BLOCK, LANES), BF16)
    stage = [pltpu.VMEM((experts * BLOCK, LANES), F32)]
    send = pl.pallas_call(
        dispatch_kernel, out_shape=packed, scratch_shapes=stage, compiler_params=params(16)
    )(ids, probs, tokens.T, cotangent.T)
    partial = pl.pallas_call(
        up_kernel,
        out_shape=jax.ShapeDtypeStruct((ROWS, 2 * hidden), BF16),
        scratch_shapes=stage,
        compiler_params=params(24),
    )(exchange(send, experts), up, down)
    share = lax.psum_scatter(partial, "tensor", scatter_dimension=0, tiled=True)
    middle = pl.pallas_call(
        middle_kernel,
        out_shape=jax.ShapeDtypeStruct((share.shape[0], 2 * hidden + LANES), BF16),
        compiler_params=params(16),
    )(share)
    joined = lax.all_gather(middle, "tensor", axis=0, tiled=True)
    back = pl.pallas_call(
        down_kernel, out_shape=packed, scratch_shapes=stage, compiler_params=params(24)
    )(joined, up, down)
    mixed, input_grad, prob_grad = pl.pallas_call(
        combine_kernel,
        out_shape=(
            jax.ShapeDtypeStruct((feat, count), BF16),
            jax.ShapeDtypeStruct((feat, count), BF16),
            jax.ShapeDtypeStruct((2, count), F32),
        ),
        scratch_shapes=stage,
        compiler_params=params(16),
    )(ids, probs, exchange(back, experts))
    return mixed.T, input_grad.T, prob_grad.T


def solution(mesh):
    return jax.shard_map(
        per_device,
        mesh=mesh,
        in_specs=(
            P("dp", "tensor"),
            P("dp", "tensor"),
            P("dp", None),
            P("dp", None),
            P("dp", "tensor", None),
            P("dp", None, "tensor"),
        ),
        out_specs=(P("dp", "tensor"), P("dp", "tensor"), P("dp", None)),
        check_vma=False,
    )
```

```python
import jax
import jax.numpy as jnp
from jax import lax
from jax.experimental import pallas as pl
from jax.experimental.pallas import tpu as pltpu
from jax.sharding import PartitionSpec as P

CAP = 3
LANES = 128
BLOCK = 24
ROWS = 320
F32 = jnp.float32
BF16 = jnp.bfloat16
MIB = 1024 * 1024


def params(mib):
    return pltpu.CompilerParams(vmem_limit_bytes=mib * MIB)


def one_hots(ids_ref, experts):
    tokens = ids_ref.shape[1]
    expert = lax.broadcasted_iota(jnp.int32, (experts, tokens), 0)
    named = [(ids_ref[k : k + 1, :] == expert).astype(F32) for k in range(2)]
    before = lax.broadcasted_iota(jnp.int32, (tokens, tokens), 0)
    after = lax.broadcasted_iota(jnp.int32, (tokens, tokens), 1)
    earlier = (before < after).astype(F32).astype(BF16)
    slot = jnp.dot((named[0] + named[1]).astype(BF16), earlier, preferred_element_type=F32)
    return named, slot


def tile_of(first, second, j):
    if j < 3:
        return first[:, j * LANES : (j + 1) * LANES]
    if j < 6:
        return second[:, (j - 3) * LANES : (j - 2) * LANES]
    return jnp.concatenate([first[:, 3 * LANES :], second[:, 3 * LANES :]], axis=1)


def pair_of(tiles):
    half = LANES // 2
    first = jnp.concatenate(tiles[0:3] + [tiles[6][:, :half]], axis=1)
    second = jnp.concatenate(tiles[3:6] + [tiles[6][:, half:]], axis=1)
    return first, second


def chunks(size, step):
    return [(at, min(at + step, size)) for at in range(0, size, step)]


def copies(sources, targets, semaphores):
    started = [
        pltpu.make_async_copy(source, target, semaphores.at[i])
        for i, (source, target) in enumerate(zip(sources, targets))
    ]
    for copy in started:
        copy.start()
    return started


def dispatch_kernel(
    ids_hbm,
    probs_hbm,
    tok_hbm,
    cot_hbm,
    up_hbm,
    down_hbm,
    out_ref,
    up_ref,
    down_ref,
    scratch,
    ids_ref,
    probs_ref,
    tok_ref,
    cot_ref,
    semaphores,
):
    experts = out_ref.shape[0] // BLOCK
    started = copies(
        (ids_hbm, probs_hbm, tok_hbm, cot_hbm, up_hbm, down_hbm),
        (ids_ref, probs_ref, tok_ref, cot_ref, up_ref, down_ref),
        semaphores,
    )
    for copy in started[:4]:
        copy.wait()
    named, slot = one_hots(ids_ref, experts)
    either = named[0] + named[1]
    weight = named[0] * probs_ref[0:1, :] + named[1] * probs_ref[1:2, :]
    across = (((1,), (1,)), ((), ()))
    for s in range(CAP):
        here = (slot == s).astype(F32)
        pick = (either * here).astype(BF16)
        rows = lax.dot_general(pick, tok_ref[...], across, preferred_element_type=F32)
        grads = lax.dot_general(pick, cot_ref[...], across, preferred_element_type=F32)
        grads = grads * jnp.sum(weight * here, axis=1, keepdims=True)
        for j in range(7):
            scratch[pl.ds(s * 7 + j, experts, stride=BLOCK), :] = tile_of(rows, grads, j)
    for r in range(7 * CAP, BLOCK):
        scratch[pl.ds(r, experts, stride=BLOCK), :] = jnp.zeros((experts, LANES), F32)
    out_ref[...] = scratch[...].astype(BF16)
    for copy in started[4:]:
        copy.wait()


def up_kernel(block_ref, up_ref, down_ref, out_hbm, scratch, out_ref, semaphores):
    sources = block_ref.shape[0] // BLOCK
    hidden = up_ref.shape[1]
    scratch[...] = block_ref[...].astype(F32)
    rows, grads = [], []
    for s in range(CAP):
        tiles = [scratch[pl.ds(s * 7 + j, sources, stride=BLOCK), :] for j in range(7)]
        first, second = pair_of(tiles)
        rows.append(first)
        grads.append(second)
    pad = jnp.zeros((ROWS - CAP * sources, up_ref.shape[0]), F32)
    rows = jnp.concatenate(rows + [pad], axis=0).astype(BF16)
    grads = jnp.concatenate(grads + [pad], axis=0).astype(BF16)
    started = []
    for left, weight, base in ((rows, up_ref, 0), (grads, down_ref, hidden)):
        for at, to in chunks(hidden, 512):
            span = slice(base + at, base + to)
            out_ref[:, span] = jnp.dot(
                left, weight[:, at:to], preferred_element_type=F32
            ).astype(BF16)
            started.append(
                pltpu.make_async_copy(
                    out_ref.at[:, span], out_hbm.at[:, span], semaphores.at[len(started)]
                )
            )
            started[-1].start()
    for copy in started:
        copy.wait()


def middle_kernel(sum_ref, out_ref):
    hidden = sum_ref.shape[1] // 2
    up_sum = sum_ref[:, :hidden].astype(F32)
    grad = sum_ref[:, hidden:].astype(F32)
    sigmoid = 1.0 / (1.0 + jnp.exp(-up_sum))
    act = (up_sum * sigmoid).astype(BF16)
    out_ref[:, :hidden] = act
    out_ref[:, hidden : 2 * hidden] = (
        grad * sigmoid * (1.0 + up_sum * (1.0 - sigmoid))
    ).astype(BF16)
    score = jnp.sum(act.astype(F32) * grad, axis=1, keepdims=True)
    high = score.astype(BF16).astype(F32)
    lane = lax.broadcasted_iota(jnp.int32, (sum_ref.shape[0], LANES), 1)
    out_ref[:, 2 * hidden :] = jnp.where(
        lane == 0, high, jnp.where(lane == 1, score - high, 0.0)
    ).astype(BF16)


def columns_at(at, to):
    return (slice(None), slice(at, to))


def down_kernel(join_hbm, up_ref, down_hbm, out_ref, scratch, join_ref, down_ref, semaphores):
    sources = out_ref.shape[0] // BLOCK
    hidden = up_ref.shape[1]
    across = (((1,), (1,)), ((), ()))
    spans = chunks(hidden, 1024)
    first = [columns_at(hidden + at, hidden + to) for at, to in spans]
    second = [columns_at(at, to) for at, to in spans]
    last = [columns_at(2 * hidden, 2 * hidden + LANES)]
    own = [columns_at(at, to) for at, to in spans]
    started = copies(
        [join_hbm.at[part] for part in first]
        + [down_hbm.at[part] for part in own]
        + [join_hbm.at[part] for part in second + last],
        [join_ref.at[part] for part in first]
        + [down_ref.at[part] for part in own]
        + [join_ref.at[part] for part in second + last],
        semaphores,
    )
    count = len(spans)
    part, out = 0.0, 0.0
    for i in range(count):
        started[i].wait()
        part += lax.dot_general(
            join_ref[first[i]], up_ref[own[i]], across, preferred_element_type=F32
        )
    for i in range(count):
        started[count + i].wait()
        started[2 * count + i].wait()
        out += lax.dot_general(
            join_ref[second[i]], down_ref[own[i]], across, preferred_element_type=F32
        )
    started[3 * count].wait()
    score = join_ref[last[0]].astype(F32)
    for s in range(CAP):
        rows = slice(s * sources, (s + 1) * sources)
        for j in range(7):
            scratch[pl.ds(s * 7 + j, sources, stride=BLOCK), :] = tile_of(out[rows], part[rows], j)
        scratch[pl.ds(7 * CAP + s, sources, stride=BLOCK), :] = score[rows]
    out_ref[...] = scratch[...].astype(BF16)


def combine_kernel(ids_ref, probs_ref, block_ref, mixed_ref, grad_ref, score_ref, scratch):
    experts = block_ref.shape[0] // BLOCK
    named, slot = one_hots(ids_ref, experts)
    scratch[...] = block_ref[...].astype(F32)
    along = (((0,), (0,)), ((), ()))
    outs, parts, picks = [], [], []
    scores = [jnp.zeros((1, ids_ref.shape[1]), F32) for _ in range(2)]
    for s in range(CAP):
        here = (slot == s).astype(F32)
        tiles = [scratch[pl.ds(s * 7 + j, experts, stride=BLOCK), :] for j in range(7)]
        first, second = pair_of(tiles)
        outs.append(first)
        parts.append(second)
        picks.append(jnp.concatenate([named[0] * here, named[1] * here], axis=1))
        tail = scratch[pl.ds(7 * CAP + s, experts, stride=BLOCK), :]
        value = tail[:, 0:1] + tail[:, 1:2]
        for k in range(2):
            scores[k] += jnp.sum(named[k] * here * value, axis=0, keepdims=True)
    outs = jnp.concatenate(outs, axis=0).astype(BF16)
    parts = jnp.concatenate(parts, axis=0).astype(BF16)
    picks = jnp.concatenate(picks, axis=0)
    tokens = ids_ref.shape[1]
    either = (picks[:, :tokens] + picks[:, tokens:]).astype(BF16)
    got = lax.dot_general(outs, picks.astype(BF16), along, preferred_element_type=F32)
    mixed_ref[...] = (
        got[:, :tokens] * probs_ref[0:1, :] + got[:, tokens:] * probs_ref[1:2, :]
    ).astype(BF16)
    grad_ref[...] = lax.dot_general(parts, either, along, preferred_element_type=F32).astype(BF16)
    score_ref[...] = jnp.concatenate(scores, axis=0) / probs_ref[...]


def in_hbm(array):
    return pltpu.with_memory_space_constraint(array, pltpu.HBM)


def exchange(block, experts):
    block = block.reshape(experts, BLOCK, LANES)
    block = lax.all_to_all(block, "dp", split_axis=0, concat_axis=0, tiled=True)
    return block.reshape(experts * BLOCK, LANES)


def per_device(tokens, cotangent, expert_ids, route_probs, up_weight, down_weight):
    count, feat = tokens.shape
    experts = lax.axis_size("dp")
    hidden = up_weight.shape[2]
    ids, probs = expert_ids.T, route_probs.T
    up, down = up_weight[0], down_weight[0].T
    packed = jax.ShapeDtypeStruct((experts * BLOCK, LANES), BF16)
    stage = [pltpu.VMEM((experts * BLOCK, LANES), F32)]
    anywhere = pl.BlockSpec(memory_space=pltpu.HBM)
    send, up_near, down_near = pl.pallas_call(
        dispatch_kernel,
        out_shape=(
            packed,
            pltpu.VMEM(up.shape, BF16),
            pltpu.VMEM(down.shape, BF16),
        ),
        in_specs=[anywhere] * 6,
        scratch_shapes=stage
        + [
            pltpu.VMEM(ids.shape, jnp.int32),
            pltpu.VMEM(probs.shape, F32),
            pltpu.VMEM((feat, count), BF16),
            pltpu.VMEM((feat, count), BF16),
            pltpu.SemaphoreType.DMA((6,)),
        ],
        compiler_params=params(14),
    )(*map(in_hbm, (ids, probs, tokens.T, cotangent.T, up, down)))
    partial = pl.pallas_call(
        up_kernel,
        out_shape=jax.ShapeDtypeStruct((ROWS, 2 * hidden), BF16),
        out_specs=anywhere,
        scratch_shapes=stage
        + [
            pltpu.VMEM((ROWS, 2 * hidden), BF16),
            pltpu.SemaphoreType.DMA((2 * len(chunks(hidden, 512)),)),
        ],
        compiler_params=params(20),
    )(exchange(send, experts), up_near, down_near)
    share = lax.psum_scatter(partial, "tensor", scatter_dimension=0, tiled=True)
    middle = pl.pallas_call(
        middle_kernel,
        out_shape=jax.ShapeDtypeStruct((share.shape[0], 2 * hidden + LANES), BF16),
        compiler_params=params(14),
    )(share)
    joined = lax.all_gather(middle, "tensor", axis=0, tiled=True)
    whole = pl.BlockSpec(memory_space=pltpu.VMEM)
    back = pl.pallas_call(
        down_kernel,
        out_shape=packed,
        in_specs=[anywhere, whole, anywhere],
        scratch_shapes=stage
        + [
            pltpu.VMEM(joined.shape, BF16),
            pltpu.VMEM(down.shape, BF16),
            pltpu.SemaphoreType.DMA((3 * len(chunks(hidden, 1024)) + 1,)),
        ],
        compiler_params=params(20),
    )(in_hbm(joined), up_near, in_hbm(down))
    mixed, input_grad, prob_grad = pl.pallas_call(
        combine_kernel,
        out_shape=(
            jax.ShapeDtypeStruct((feat, count), BF16),
            jax.ShapeDtypeStruct((feat, count), BF16),
            jax.ShapeDtypeStruct((2, count), F32),
        ),
        scratch_shapes=stage,
        compiler_params=params(14),
    )(ids, probs, exchange(back, experts))
    return mixed.T, input_grad.T, prob_grad.T


def solution(mesh):
    return jax.shard_map(
        per_device,
        mesh=mesh,
        in_specs=(
            P("dp", "tensor"),
            P("dp", "tensor"),
            P("dp", None),
            P("dp", None),
            P("dp", "tensor", None),
            P("dp", None, "tensor"),
        ),
        out_specs=(P("dp", "tensor"), P("dp", "tensor"), P("dp", None)),
        check_vma=False,
    )
```

```python
import functools

import jax
import jax.numpy as jnp
from jax import lax
from jax.experimental import pallas as pl
from jax.experimental.pallas import tpu as pltpu
from jax.sharding import PartitionSpec as P

CAP = 3
LANES = 128
BLOCK = 24
SHARE = 40
HEAD = 16
SMALL = 8
LARGE = 16
F32 = jnp.float32
BF16 = jnp.bfloat16
MIB = 1024 * 1024


def params(mib):
    return pltpu.CompilerParams(vmem_limit_bytes=mib * MIB)


def one_hots(ids_ref, experts):
    tokens = ids_ref.shape[1]
    expert = lax.broadcasted_iota(jnp.int32, (experts, tokens), 0)
    named = [(ids_ref[k : k + 1, :] == expert).astype(F32) for k in range(2)]
    before = lax.broadcasted_iota(jnp.int32, (tokens, tokens), 0)
    after = lax.broadcasted_iota(jnp.int32, (tokens, tokens), 1)
    earlier = (before < after).astype(F32).astype(BF16)
    slot = jnp.dot((named[0] + named[1]).astype(BF16), earlier, preferred_element_type=F32)
    return named, slot


def tile_of(first, second, j):
    if j < 3:
        return first[:, j * LANES : (j + 1) * LANES]
    if j < 6:
        return second[:, (j - 3) * LANES : (j - 2) * LANES]
    return jnp.concatenate([first[:, 3 * LANES :], second[:, 3 * LANES :]], axis=1)


def pair_of(tiles):
    half = LANES // 2
    first = jnp.concatenate(tiles[0:3] + [tiles[6][:, :half]], axis=1)
    second = jnp.concatenate(tiles[3:6] + [tiles[6][:, half:]], axis=1)
    return first, second


def chunks(size, step):
    return [(at, min(at + step, size)) for at in range(0, size, step)]


def copies(sources, targets, semaphores):
    started = [
        pltpu.make_async_copy(source, target, semaphores.at[i])
        for i, (source, target) in enumerate(zip(sources, targets))
    ]
    for copy in started:
        copy.start()
    return started


def dispatch_kernel(
    ids_hbm,
    probs_hbm,
    tok_hbm,
    cot_hbm,
    up_hbm,
    down_hbm,
    out_ref,
    up_ref,
    down_ref,
    scratch,
    ids_ref,
    probs_ref,
    tok_ref,
    cot_ref,
    semaphores,
):
    experts = out_ref.shape[0] // BLOCK
    started = copies(
        (ids_hbm, probs_hbm, tok_hbm, cot_hbm, up_hbm, down_hbm),
        (ids_ref, probs_ref, tok_ref, cot_ref, up_ref, down_ref),
        semaphores,
    )
    for copy in started[:4]:
        copy.wait()
    named, slot = one_hots(ids_ref, experts)
    either = named[0] + named[1]
    weight = named[0] * probs_ref[0:1, :] + named[1] * probs_ref[1:2, :]
    across = (((1,), (1,)), ((), ()))
    for s in range(CAP):
        here = (slot == s).astype(F32)
        pick = (either * here).astype(BF16)
        rows = lax.dot_general(pick, tok_ref[...], across, preferred_element_type=F32)
        grads = lax.dot_general(pick, cot_ref[...], across, preferred_element_type=F32)
        grads = grads * jnp.sum(weight * here, axis=1, keepdims=True)
        for j in range(7):
            scratch[pl.ds(s * 7 + j, experts, stride=BLOCK), :] = tile_of(rows, grads, j)
    for r in range(7 * CAP, BLOCK):
        scratch[pl.ds(r, experts, stride=BLOCK), :] = jnp.zeros((experts, LANES), F32)
    out_ref[...] = scratch[...].astype(BF16)
    for copy in started[4:]:
        copy.wait()


def row_of(device, slot, each):
    return device * SHARE + (HEAD + (slot - 1) * each if slot else 0)


def up_kernel(
    block_ref, up_ref, down_ref, out_hbm, scratch, row_ref, grad_ref, out_ref, semaphores
):
    sources = block_ref.shape[0] // BLOCK
    feat, hidden = up_ref.shape
    devices = out_ref.shape[0] // SHARE
    each = sources // devices
    scratch[...] = block_ref[...].astype(F32)
    for d in range(devices):
        for s in range(CAP):
            rows = slice(row_of(d, s, each), row_of(d, s, each) + each)
            for j in range(7):
                tile = scratch[pl.ds(d * each * BLOCK + s * 7 + j, each, stride=BLOCK), :]
                if j < 3:
                    row_ref[rows, j * LANES : (j + 1) * LANES] = tile
                elif j < 6:
                    grad_ref[rows, (j - 3) * LANES : (j - 2) * LANES] = tile
                else:
                    row_ref[rows, 3 * LANES :] = tile
        pad = slice(d * SHARE + each, d * SHARE + HEAD)
        row_ref[pad, :] = jnp.zeros((HEAD - each, row_ref.shape[1]), F32)
        grad_ref[pad, :] = jnp.zeros((HEAD - each, grad_ref.shape[1]), F32)
    rows = row_ref[:, :feat].astype(BF16)
    grads = jnp.concatenate([grad_ref[...], row_ref[:, feat:]], axis=1).astype(BF16)
    started = []
    for left, weight, base in ((rows, up_ref, 0), (grads, down_ref, hidden)):
        for at, to in chunks(hidden, 512):
            span = slice(base + at, base + to)
            out_ref[:, span] = jnp.dot(
                left, weight[:, at:to], preferred_element_type=F32
            ).astype(BF16)
            started.append(
                pltpu.make_async_copy(
                    out_ref.at[:, span], out_hbm.at[:, span], semaphores.at[len(started)]
                )
            )
            started[-1].start()
    for copy in started:
        copy.wait()


def middle_kernel(sum_ref, small_ref, large_ref, scratch):
    hidden = sum_ref.shape[1] // 2
    each = small_ref.shape[0] // 2
    up_sum = sum_ref[:, :hidden].astype(F32)
    grad = sum_ref[:, hidden:].astype(F32)
    sigmoid = 1.0 / (1.0 + jnp.exp(-up_sum))
    act = (up_sum * sigmoid).astype(BF16).astype(F32)
    up_grad = grad * sigmoid * (1.0 + up_sum * (1.0 - sigmoid))
    score = jnp.sum(act * grad, axis=1, keepdims=True)
    high = score.astype(BF16).astype(F32)
    lane = lax.broadcasted_iota(jnp.int32, (sum_ref.shape[0], LANES), 1)
    score = jnp.where(lane == 0, high, jnp.where(lane == 1, score - high, 0.0))
    scratch[:each, :hidden] = act[:each]
    scratch[each:, :hidden] = up_grad[:each]
    scratch[:each, hidden:] = score[:each]
    scratch[each:, hidden:] = jnp.zeros((each, LANES), F32)
    small_ref[...] = scratch[...].astype(BF16)
    rest = slice(HEAD, HEAD + 2 * each)
    large_ref[:, :hidden] = act[rest].astype(BF16)
    large_ref[:, hidden : 2 * hidden] = up_grad[rest].astype(BF16)
    large_ref[:, 2 * hidden :] = score[rest].astype(BF16)


def columns_at(at, to):
    return (slice(None), slice(at, to))


def pack(out_ref, part_ref, scores, target, rows, devices, each, slots, height):
    for d in range(devices):
        for s in range(slots):
            low, high = rows(d, s)
            left = slice(low, low + each)
            right = slice(high, high + each)
            out, part = out_ref[left, :], part_ref[right, :]
            for j in range(7):
                target[pl.ds(d * each * height + s * 7 + j, each, stride=height), :] = tile_of(
                    out, part, j
                )
            target[pl.ds(d * each * height + 7 * slots + s, each, stride=height), :] = scores[
                left, :
            ]


def down_small_kernel(
    devices,
    join_hbm,
    up_ref,
    down_hbm,
    out_ref,
    target,
    join_ref,
    down_ref,
    out_rows,
    part_rows,
    score_rows,
    semaphores,
):
    hidden = up_ref.shape[1]
    across = (((1,), (1,)), ((), ()))
    started = copies((join_hbm, down_hbm), (join_ref, down_ref), semaphores)
    started[0].wait()
    joined = join_ref[:, :hidden]
    part_rows[...] = lax.dot_general(joined, up_ref[...], across, preferred_element_type=F32)
    score_rows[...] = join_ref[:, hidden:].astype(F32)
    started[1].wait()
    out_rows[...] = lax.dot_general(joined, down_ref[...], across, preferred_element_type=F32)
    each = join_ref.shape[0] // devices // 2
    pack(
        out_rows,
        part_rows,
        score_rows,
        target,
        lambda d, s: (2 * each * d, 2 * each * d + each),
        devices,
        each,
        1,
        SMALL,
    )
    out_ref[...] = target[...].astype(BF16)


def down_large_kernel(
    devices,
    join_hbm,
    up_ref,
    down_hbm,
    out_ref,
    target,
    join_ref,
    down_ref,
    out_rows,
    part_rows,
    score_rows,
    semaphores,
):
    hidden = up_ref.shape[1]
    across = (((1,), (1,)), ((), ()))
    spans = chunks(hidden, 1024)
    parts = [columns_at(base + at, base + to) for base in (hidden, 0) for at, to in spans]
    parts.append(columns_at(2 * hidden, 2 * hidden + LANES))
    own = [columns_at(at, to) for at, to in spans]
    count = len(spans)
    from_join = copies(
        [join_hbm.at[part] for part in parts[:count]],
        [join_ref.at[part] for part in parts[:count]],
        semaphores,
    )
    from_down = copies(
        [down_hbm.at[part] for part in own],
        [down_ref.at[part] for part in own],
        semaphores.at[pl.ds(count, count)],
    )
    started = copies(
        [join_hbm.at[part] for part in parts[count:]],
        [join_ref.at[part] for part in parts[count:]],
        semaphores.at[pl.ds(2 * count, count + 1)],
    )
    total = 0.0
    for i in range(count):
        from_join[i].wait()
        total += lax.dot_general(
            join_ref[parts[i]], up_ref[own[i]], across, preferred_element_type=F32
        )
    part_rows[...] = total
    total = 0.0
    for i in range(count):
        from_down[i].wait()
        started[i].wait()
        total += lax.dot_general(
            join_ref[parts[count + i]], down_ref[own[i]], across, preferred_element_type=F32
        )
    out_rows[...] = total
    started[-1].wait()
    score_rows[...] = join_ref[parts[-1]].astype(F32)
    each = join_ref.shape[0] // devices // 2

    def rows(d, s):
        return ((2 * d + s) * each,) * 2

    pack(
        out_rows, part_rows, score_rows, target, rows, devices, each, 2, LARGE
    )
    out_ref[...] = target[...].astype(BF16)


def combine_kernel(
    ids_ref, probs_ref, small_ref, large_ref, mixed_ref, grad_ref, score_ref, first_rows, rest_rows
):
    experts = small_ref.shape[0] // SMALL
    named, slot = one_hots(ids_ref, experts)
    first_rows[...] = small_ref[...].astype(F32)
    rest_rows[...] = large_ref[...].astype(F32)

    def came(slot, j):
        if slot == 0:
            return first_rows[pl.ds(j, experts, stride=SMALL), :]
        at = (slot - 1) * 7 + j if j < 7 else 14 + slot - 1
        return rest_rows[pl.ds(at, experts, stride=LARGE), :]

    along = (((0,), (0,)), ((), ()))
    outs, parts, picks = [], [], []
    scores = [jnp.zeros((1, ids_ref.shape[1]), F32) for _ in range(2)]
    for s in range(CAP):
        here = (slot == s).astype(F32)
        first, second = pair_of([came(s, j) for j in range(7)])
        outs.append(first)
        parts.append(second)
        picks.append(jnp.concatenate([named[0] * here, named[1] * here], axis=1))
        tail = came(s, 7)
        value = tail[:, 0:1] + tail[:, 1:2]
        for k in range(2):
            scores[k] += jnp.sum(named[k] * here * value, axis=0, keepdims=True)
    outs = jnp.concatenate(outs, axis=0).astype(BF16)
    parts = jnp.concatenate(parts, axis=0).astype(BF16)
    picks = jnp.concatenate(picks, axis=0)
    tokens = ids_ref.shape[1]
    either = (picks[:, :tokens] + picks[:, tokens:]).astype(BF16)
    got = lax.dot_general(outs, picks.astype(BF16), along, preferred_element_type=F32)
    mixed_ref[...] = (
        got[:, :tokens] * probs_ref[0:1, :] + got[:, tokens:] * probs_ref[1:2, :]
    ).astype(BF16)
    grad_ref[...] = lax.dot_general(parts, either, along, preferred_element_type=F32).astype(BF16)
    score_ref[...] = jnp.concatenate(scores, axis=0) / probs_ref[...]


def in_hbm(array):
    return pltpu.with_memory_space_constraint(array, pltpu.HBM)


def exchange(block, experts):
    shape = block.shape
    block = block.reshape(experts, -1, LANES)
    block = lax.all_to_all(block, "dp", split_axis=0, concat_axis=0, tiled=True)
    return block.reshape(shape)


def per_device(tokens, cotangent, expert_ids, route_probs, up_weight, down_weight):
    count, feat = tokens.shape
    experts = lax.axis_size("dp")
    hidden = up_weight.shape[2]
    ids, probs = expert_ids.T, route_probs.T
    up, down = up_weight[0], down_weight[0].T
    packed = jax.ShapeDtypeStruct((experts * BLOCK, LANES), BF16)
    stage = [pltpu.VMEM((experts * BLOCK, LANES), F32)]
    anywhere = pl.BlockSpec(memory_space=pltpu.HBM)
    send, up_near, down_near = pl.pallas_call(
        dispatch_kernel,
        out_shape=(
            packed,
            pltpu.VMEM(up.shape, BF16),
            pltpu.VMEM(down.shape, BF16),
        ),
        in_specs=[anywhere] * 6,
        scratch_shapes=stage
        + [
            pltpu.VMEM(ids.shape, jnp.int32),
            pltpu.VMEM(probs.shape, F32),
            pltpu.VMEM((feat, count), BF16),
            pltpu.VMEM((feat, count), BF16),
            pltpu.SemaphoreType.DMA((6,)),
        ],
        compiler_params=params(14),
    )(*map(in_hbm, (ids, probs, tokens.T, cotangent.T, up, down)))
    devices = lax.axis_size("tensor")
    each = experts // devices
    partial = pl.pallas_call(
        up_kernel,
        out_shape=pltpu.HBM((devices * SHARE, 2 * hidden), BF16),
        out_specs=anywhere,
        scratch_shapes=stage
        + [
            pltpu.VMEM((devices * SHARE, 4 * LANES), F32),
            pltpu.VMEM((devices * SHARE, 3 * LANES), F32),
            pltpu.VMEM((devices * SHARE, 2 * hidden), BF16),
            pltpu.SemaphoreType.DMA((2 * len(chunks(hidden, 512)),)),
        ],
        compiler_params=params(20),
    )(exchange(send, experts), up_near, down_near)
    share = lax.psum_scatter(partial, "tensor", scatter_dimension=0, tiled=True)
    small, large = pl.pallas_call(
        middle_kernel,
        out_shape=(
            jax.ShapeDtypeStruct((2 * each, hidden + LANES), BF16),
            jax.ShapeDtypeStruct((2 * each, 2 * hidden + LANES), BF16),
        ),
        scratch_shapes=[pltpu.VMEM((2 * each, hidden + LANES), F32)],
        compiler_params=params(14),
    )(share)
    whole = pl.BlockSpec(memory_space=pltpu.VMEM)
    joined = lax.all_gather(large, "tensor", axis=0, tiled=True)
    joined_small = lax.all_gather(small, "tensor", axis=0, tiled=True)
    products = [
        pltpu.VMEM((2 * each * devices, feat), F32),
        pltpu.VMEM((2 * each * devices, feat), F32),
        pltpu.VMEM((2 * each * devices, LANES), F32),
    ]
    back_small = pl.pallas_call(
        functools.partial(down_small_kernel, devices),
        out_shape=jax.ShapeDtypeStruct((experts * SMALL, LANES), BF16),
        in_specs=[anywhere, whole, anywhere],
        scratch_shapes=[
            pltpu.VMEM((experts * SMALL, LANES), F32),
            pltpu.VMEM(joined_small.shape, BF16),
            pltpu.VMEM(down.shape, BF16),
        ]
        + products
        + [pltpu.SemaphoreType.DMA((2,))],
        compiler_params=params(20),
    )(in_hbm(joined_small), up_near, in_hbm(down))
    back_small = exchange(back_small, experts)
    back = pl.pallas_call(
        functools.partial(down_large_kernel, devices),
        out_shape=jax.ShapeDtypeStruct((experts * LARGE, LANES), BF16),
        in_specs=[anywhere, whole, anywhere],
        scratch_shapes=[
            pltpu.VMEM((experts * LARGE, LANES), F32),
            pltpu.VMEM(joined.shape, BF16),
            pltpu.VMEM(down.shape, BF16),
        ]
        + products
        + [pltpu.SemaphoreType.DMA((3 * len(chunks(hidden, 1024)) + 1,))],
        compiler_params=params(20),
    )(in_hbm(joined), up_near, in_hbm(down))
    mixed, input_grad, prob_grad = pl.pallas_call(
        combine_kernel,
        out_shape=(
            jax.ShapeDtypeStruct((feat, count), BF16),
            jax.ShapeDtypeStruct((feat, count), BF16),
            jax.ShapeDtypeStruct((2, count), F32),
        ),
        scratch_shapes=[
            pltpu.VMEM((experts * SMALL, LANES), F32),
            pltpu.VMEM((experts * LARGE, LANES), F32),
        ],
        compiler_params=params(14),
    )(ids, probs, back_small, exchange(back, experts))
    return mixed.T, input_grad.T, prob_grad.T


def solution(mesh):
    return jax.shard_map(
        per_device,
        mesh=mesh,
        in_specs=(
            P("dp", "tensor"),
            P("dp", "tensor"),
            P("dp", None),
            P("dp", None),
            P("dp", "tensor", None),
            P("dp", None, "tensor"),
        ),
        out_specs=(P("dp", "tensor"), P("dp", "tensor"), P("dp", None)),
        check_vma=False,
    )
```

```python
import functools

import jax
import jax.numpy as jnp
from jax import lax
from jax.experimental import pallas as pl
from jax.experimental.pallas import tpu as pltpu
from jax.sharding import PartitionSpec as P

CAP = 3
LANES = 128
BLOCK = 24
SHARE = 40
HEAD = 16
SMALL = 8
LARGE = 16
F32 = jnp.float32
BF16 = jnp.bfloat16
MIB = 1024 * 1024


def params(mib):
    return pltpu.CompilerParams(vmem_limit_bytes=mib * MIB)


def one_hots(ids_ref, experts):
    tokens = ids_ref.shape[1]
    expert = lax.broadcasted_iota(jnp.int32, (experts, tokens), 0)
    named = [(ids_ref[k : k + 1, :] == expert).astype(F32) for k in range(2)]
    before = lax.broadcasted_iota(jnp.int32, (tokens, tokens), 0)
    after = lax.broadcasted_iota(jnp.int32, (tokens, tokens), 1)
    earlier = (before < after).astype(F32).astype(BF16)
    slot = jnp.dot((named[0] + named[1]).astype(BF16), earlier, preferred_element_type=F32)
    return named, slot


def tile_of(first, second, j):
    if j < 3:
        return first[:, j * LANES : (j + 1) * LANES]
    if j < 6:
        return second[:, (j - 3) * LANES : (j - 2) * LANES]
    return jnp.concatenate([first[:, 3 * LANES :], second[:, 3 * LANES :]], axis=1)


def pair_of(tiles):
    half = LANES // 2
    first = jnp.concatenate(tiles[0:3] + [tiles[6][:, :half]], axis=1)
    second = jnp.concatenate(tiles[3:6] + [tiles[6][:, half:]], axis=1)
    return first, second


def chunks(size, step):
    return [(at, min(at + step, size)) for at in range(0, size, step)]


def copies(sources, targets, semaphores):
    started = [
        pltpu.make_async_copy(source, target, semaphores.at[i])
        for i, (source, target) in enumerate(zip(sources, targets))
    ]
    for copy in started:
        copy.start()
    return started


def dispatch_kernel(
    ids_hbm,
    probs_hbm,
    tok_hbm,
    cot_hbm,
    up_hbm,
    down_hbm,
    out_ref,
    up_ref,
    down_ref,
    scratch,
    ids_ref,
    probs_ref,
    tok_ref,
    cot_ref,
    semaphores,
):
    experts = out_ref.shape[0] // BLOCK
    started = copies(
        (ids_hbm, probs_hbm, tok_hbm, cot_hbm, up_hbm, down_hbm),
        (ids_ref, probs_ref, tok_ref, cot_ref, up_ref, down_ref),
        semaphores,
    )
    for copy in started[:4]:
        copy.wait()
    named, slot = one_hots(ids_ref, experts)
    either = named[0] + named[1]
    weight = named[0] * probs_ref[0:1, :] + named[1] * probs_ref[1:2, :]
    across = (((1,), (1,)), ((), ()))
    for s in range(CAP):
        here = (slot == s).astype(F32)
        pick = (either * here).astype(BF16)
        rows = lax.dot_general(pick, tok_ref[...], across, preferred_element_type=F32)
        grads = lax.dot_general(pick, cot_ref[...], across, preferred_element_type=F32)
        grads = grads * jnp.sum(weight * here, axis=1, keepdims=True)
        for j in range(7):
            scratch[pl.ds(s * 7 + j, experts, stride=BLOCK), :] = tile_of(rows, grads, j)
    for r in range(7 * CAP, BLOCK):
        scratch[pl.ds(r, experts, stride=BLOCK), :] = jnp.zeros((experts, LANES), F32)
    out_ref[...] = scratch[...].astype(BF16)
    for copy in started[4:]:
        copy.wait()


def row_of(device, slot, each):
    return device * SHARE + (HEAD + (slot - 1) * each if slot else 0)


def up_kernel(
    block_ref, up_ref, down_ref, out_hbm, scratch, row_ref, grad_ref, out_ref, semaphores
):
    sources = block_ref.shape[0] // BLOCK
    feat, hidden = up_ref.shape
    devices = out_ref.shape[0] // SHARE
    each = sources // devices
    scratch[...] = block_ref[...].astype(F32)
    for d in range(devices):
        for s in range(CAP):
            rows = slice(row_of(d, s, each), row_of(d, s, each) + each)
            for j in range(7):
                tile = scratch[pl.ds(d * each * BLOCK + s * 7 + j, each, stride=BLOCK), :]
                if j < 3:
                    row_ref[rows, j * LANES : (j + 1) * LANES] = tile
                elif j < 6:
                    grad_ref[rows, (j - 3) * LANES : (j - 2) * LANES] = tile
                else:
                    row_ref[rows, 3 * LANES :] = tile
        pad = slice(d * SHARE + each, d * SHARE + HEAD)
        row_ref[pad, :] = jnp.zeros((HEAD - each, row_ref.shape[1]), F32)
        grad_ref[pad, :] = jnp.zeros((HEAD - each, grad_ref.shape[1]), F32)
    rows = row_ref[:, :feat].astype(BF16)
    grads = jnp.concatenate([grad_ref[...], row_ref[:, feat:]], axis=1).astype(BF16)
    started = []
    for left, weight, base in ((rows, up_ref, 0), (grads, down_ref, hidden)):
        for at, to in chunks(hidden, 512):
            span = slice(base + at, base + to)
            out_ref[:, span] = jnp.dot(
                left, weight[:, at:to], preferred_element_type=F32
            ).astype(BF16)
            started.append(
                pltpu.make_async_copy(
                    out_ref.at[:, span], out_hbm.at[:, span], semaphores.at[len(started)]
                )
            )
            started[-1].start()
    for copy in started:
        copy.wait()


def middle_kernel(sum_ref, small_ref, large_ref, scratch):
    hidden = sum_ref.shape[1] // 2
    each = small_ref.shape[0] // 2
    up_sum = sum_ref[:, :hidden].astype(F32)
    grad = sum_ref[:, hidden:].astype(F32)
    sigmoid = 1.0 / (1.0 + jnp.exp(-up_sum))
    act = (up_sum * sigmoid).astype(BF16).astype(F32)
    up_grad = grad * sigmoid * (1.0 + up_sum * (1.0 - sigmoid))
    score = jnp.sum(act * grad, axis=1, keepdims=True)
    high = score.astype(BF16).astype(F32)
    lane = lax.broadcasted_iota(jnp.int32, (sum_ref.shape[0], LANES), 1)
    score = jnp.where(lane == 0, high, jnp.where(lane == 1, score - high, 0.0))
    scratch[:each, :hidden] = act[:each]
    scratch[each:, :hidden] = up_grad[:each]
    scratch[:each, hidden:] = score[:each]
    scratch[each:, hidden:] = jnp.zeros((each, LANES), F32)
    small_ref[...] = scratch[...].astype(BF16)
    rest = slice(HEAD, HEAD + 2 * each)
    large_ref[:, :hidden] = act[rest].astype(BF16)
    large_ref[:, hidden : 2 * hidden] = up_grad[rest].astype(BF16)
    large_ref[:, 2 * hidden :] = score[rest].astype(BF16)


def columns_at(at, to):
    return (slice(None), slice(at, to))


def pack(out_ref, part_ref, scores, target, rows, devices, each, slots, height):
    for d in range(devices):
        for s in range(slots):
            low, high = rows(d, s)
            left = slice(low, low + each)
            right = slice(high, high + each)
            out, part = out_ref[left, :], part_ref[right, :]
            for j in range(7):
                target[pl.ds(d * each * height + s * 7 + j, each, stride=height), :] = tile_of(
                    out, part, j
                )
            target[pl.ds(d * each * height + 7 * slots + s, each, stride=height), :] = scores[
                left, :
            ]


def down_small_kernel(
    devices,
    join_hbm,
    up_ref,
    down_hbm,
    out_ref,
    target,
    join_ref,
    down_ref,
    out_rows,
    part_rows,
    score_rows,
    semaphores,
):
    hidden = up_ref.shape[1]
    across = (((1,), (1,)), ((), ()))
    started = copies((join_hbm, down_hbm), (join_ref, down_ref), semaphores)
    started[0].wait()
    joined = join_ref[:, :hidden]
    part_rows[...] = lax.dot_general(joined, up_ref[...], across, preferred_element_type=F32)
    score_rows[...] = join_ref[:, hidden:].astype(F32)
    started[1].wait()
    out_rows[...] = lax.dot_general(joined, down_ref[...], across, preferred_element_type=F32)
    each = join_ref.shape[0] // devices // 2
    pack(
        out_rows,
        part_rows,
        score_rows,
        target,
        lambda d, s: (2 * each * d, 2 * each * d + each),
        devices,
        each,
        1,
        SMALL,
    )
    out_ref[...] = target[...].astype(BF16)


def down_large_kernel(
    devices,
    join_hbm,
    up_ref,
    down_hbm,
    _,
    out_ref,
    target,
    join_ref,
    down_ref,
    out_rows,
    part_rows,
    score_rows,
    semaphores,
):
    hidden = up_ref.shape[1]
    across = (((1,), (1,)), ((), ()))
    spans = chunks(hidden, 1024)
    parts = [columns_at(base + at, base + to) for base in (hidden, 0) for at, to in spans]
    parts.append(columns_at(2 * hidden, 2 * hidden + LANES))
    own = [columns_at(at, to) for at, to in spans]
    count = len(spans)
    from_join = copies(
        [join_hbm.at[part] for part in parts[:count]],
        [join_ref.at[part] for part in parts[:count]],
        semaphores,
    )
    from_down = copies(
        [down_hbm.at[part] for part in own],
        [down_ref.at[part] for part in own],
        semaphores.at[pl.ds(count, count)],
    )
    started = copies(
        [join_hbm.at[part] for part in parts[count:]],
        [join_ref.at[part] for part in parts[count:]],
        semaphores.at[pl.ds(2 * count, count + 1)],
    )
    total = 0.0
    for i in range(count):
        from_join[i].wait()
        total += lax.dot_general(
            join_ref[parts[i]], up_ref[own[i]], across, preferred_element_type=F32
        )
    part_rows[...] = total
    total = 0.0
    for i in range(count):
        from_down[i].wait()
        started[i].wait()
        total += lax.dot_general(
            join_ref[parts[count + i]], down_ref[own[i]], across, preferred_element_type=F32
        )
    out_rows[...] = total
    started[-1].wait()
    score_rows[...] = join_ref[parts[-1]].astype(F32)
    each = join_ref.shape[0] // devices // 2

    def rows(d, s):
        return ((2 * d + s) * each,) * 2

    pack(
        out_rows, part_rows, score_rows, target, rows, devices, each, 2, LARGE
    )
    out_ref[...] = target[...].astype(BF16)


def combine_kernel(
    ids_ref, probs_ref, small_ref, large_ref, mixed_ref, grad_ref, score_ref, first_rows, rest_rows
):
    experts = small_ref.shape[0] // SMALL
    named, slot = one_hots(ids_ref, experts)
    first_rows[...] = small_ref[...].astype(F32)
    rest_rows[...] = large_ref[...].astype(F32)

    def came(slot, j):
        if slot == 0:
            return first_rows[pl.ds(j, experts, stride=SMALL), :]
        at = (slot - 1) * 7 + j if j < 7 else 14 + slot - 1
        return rest_rows[pl.ds(at, experts, stride=LARGE), :]

    along = (((0,), (0,)), ((), ()))
    outs, parts, picks = [], [], []
    scores = [jnp.zeros((1, ids_ref.shape[1]), F32) for _ in range(2)]
    for s in range(CAP):
        here = (slot == s).astype(F32)
        first, second = pair_of([came(s, j) for j in range(7)])
        outs.append(first)
        parts.append(second)
        picks.append(jnp.concatenate([named[0] * here, named[1] * here], axis=1))
        tail = came(s, 7)
        value = tail[:, 0:1] + tail[:, 1:2]
        for k in range(2):
            scores[k] += jnp.sum(named[k] * here * value, axis=0, keepdims=True)
    outs = jnp.concatenate(outs, axis=0).astype(BF16)
    parts = jnp.concatenate(parts, axis=0).astype(BF16)
    picks = jnp.concatenate(picks, axis=0)
    tokens = ids_ref.shape[1]
    either = (picks[:, :tokens] + picks[:, tokens:]).astype(BF16)
    got = lax.dot_general(outs, picks.astype(BF16), along, preferred_element_type=F32)
    mixed_ref[...] = (
        got[:, :tokens] * probs_ref[0:1, :] + got[:, tokens:] * probs_ref[1:2, :]
    ).astype(BF16)
    grad_ref[...] = lax.dot_general(parts, either, along, preferred_element_type=F32).astype(BF16)
    score_ref[...] = jnp.concatenate(scores, axis=0) / probs_ref[...]


def in_hbm(array):
    return pltpu.with_memory_space_constraint(array, pltpu.HBM)


def exchange(block, experts):
    shape = block.shape
    block = block.reshape(experts, -1, LANES)
    block = lax.all_to_all(block, "dp", split_axis=0, concat_axis=0, tiled=True)
    return block.reshape(shape)


def per_device(tokens, cotangent, expert_ids, route_probs, up_weight, down_weight):
    count, feat = tokens.shape
    experts = lax.axis_size("dp")
    hidden = up_weight.shape[2]
    ids, probs = expert_ids.T, route_probs.T
    up, down = up_weight[0], down_weight[0].T
    packed = jax.ShapeDtypeStruct((experts * BLOCK, LANES), BF16)
    stage = [pltpu.VMEM((experts * BLOCK, LANES), F32)]
    anywhere = pl.BlockSpec(memory_space=pltpu.HBM)
    send, up_near, down_near = pl.pallas_call(
        dispatch_kernel,
        out_shape=(
            packed,
            pltpu.VMEM(up.shape, BF16),
            pltpu.VMEM(down.shape, BF16),
        ),
        in_specs=[anywhere] * 6,
        scratch_shapes=stage
        + [
            pltpu.VMEM(ids.shape, jnp.int32),
            pltpu.VMEM(probs.shape, F32),
            pltpu.VMEM((feat, count), BF16),
            pltpu.VMEM((feat, count), BF16),
            pltpu.SemaphoreType.DMA((6,)),
        ],
        compiler_params=params(14),
    )(*map(in_hbm, (ids, probs, tokens.T, cotangent.T, up, down)))
    devices = lax.axis_size("tensor")
    each = experts // devices
    partial = pl.pallas_call(
        up_kernel,
        out_shape=pltpu.HBM((devices * SHARE, 2 * hidden), BF16),
        out_specs=anywhere,
        scratch_shapes=stage
        + [
            pltpu.VMEM((devices * SHARE, 4 * LANES), F32),
            pltpu.VMEM((devices * SHARE, 3 * LANES), F32),
            pltpu.VMEM((devices * SHARE, 2 * hidden), BF16),
            pltpu.SemaphoreType.DMA((2 * len(chunks(hidden, 512)),)),
        ],
        compiler_params=params(20),
    )(exchange(send, experts), up_near, down_near)
    share = lax.psum_scatter(partial, "tensor", scatter_dimension=0, tiled=True)
    small, large = pl.pallas_call(
        middle_kernel,
        out_shape=(
            jax.ShapeDtypeStruct((2 * each, hidden + LANES), BF16),
            jax.ShapeDtypeStruct((2 * each, 2 * hidden + LANES), BF16),
        ),
        scratch_shapes=[pltpu.VMEM((2 * each, hidden + LANES), F32)],
        compiler_params=params(14),
    )(share)
    whole = pl.BlockSpec(memory_space=pltpu.VMEM)
    joined = lax.all_gather(large, "tensor", axis=0, tiled=True)
    joined_small = lax.all_gather(small, "tensor", axis=0, tiled=True)
    products = [
        pltpu.VMEM((2 * each * devices, feat), F32),
        pltpu.VMEM((2 * each * devices, feat), F32),
        pltpu.VMEM((2 * each * devices, LANES), F32),
    ]
    back_small = pl.pallas_call(
        functools.partial(down_small_kernel, devices),
        out_shape=jax.ShapeDtypeStruct((experts * SMALL, LANES), BF16),
        in_specs=[anywhere, whole, anywhere],
        scratch_shapes=[
            pltpu.VMEM((experts * SMALL, LANES), F32),
            pltpu.VMEM(joined_small.shape, BF16),
            pltpu.VMEM(down.shape, BF16),
        ]
        + products
        + [pltpu.SemaphoreType.DMA((2,))],
        compiler_params=params(20),
    )(in_hbm(joined_small), up_near, in_hbm(down))
    back_small = exchange(back_small, experts)
    back = pl.pallas_call(
        functools.partial(down_large_kernel, devices),
        out_shape=jax.ShapeDtypeStruct((experts * LARGE, LANES), BF16),
        in_specs=[anywhere, whole, anywhere, pl.BlockSpec(memory_space=pl.ANY)],
        scratch_shapes=[
            pltpu.VMEM((experts * LARGE, LANES), F32),
            pltpu.VMEM(joined.shape, BF16),
            pltpu.VMEM(down.shape, BF16),
        ]
        + products
        + [pltpu.SemaphoreType.DMA((3 * len(chunks(hidden, 1024)) + 1,))],
        compiler_params=params(20),
    )(in_hbm(joined), up_near, in_hbm(down), back_small)
    mixed, input_grad, prob_grad = pl.pallas_call(
        combine_kernel,
        out_shape=(
            jax.ShapeDtypeStruct((feat, count), BF16),
            jax.ShapeDtypeStruct((feat, count), BF16),
            jax.ShapeDtypeStruct((2, count), F32),
        ),
        scratch_shapes=[
            pltpu.VMEM((experts * SMALL, LANES), F32),
            pltpu.VMEM((experts * LARGE, LANES), F32),
        ],
        compiler_params=params(14),
    )(ids, probs, back_small, exchange(back, experts))
    return mixed.T, input_grad.T, prob_grad.T


def solution(mesh):
    return jax.shard_map(
        per_device,
        mesh=mesh,
        in_specs=(
            P("dp", "tensor"),
            P("dp", "tensor"),
            P("dp", None),
            P("dp", None),
            P("dp", "tensor", None),
            P("dp", None, "tensor"),
        ),
        out_specs=(P("dp", "tensor"), P("dp", "tensor"), P("dp", None)),
        check_vma=False,
    )
```

```python
import functools

import jax
import jax.numpy as jnp
from jax import lax
from jax.experimental import pallas as pl
from jax.experimental.pallas import tpu as pltpu
from jax.sharding import PartitionSpec as P

CAP = 3
LANES = 128
BLOCK = 24
SHARE = 40
HEAD = 16
SMALL = 8
LARGE = 16
F32 = jnp.float32
BF16 = jnp.bfloat16
MIB = 1024 * 1024


def params(mib):
    return pltpu.CompilerParams(vmem_limit_bytes=mib * MIB)


def one_hots(ids_ref, experts):
    tokens = ids_ref.shape[1]
    expert = lax.broadcasted_iota(jnp.int32, (experts, tokens), 0)
    named = [(ids_ref[k : k + 1, :] == expert).astype(F32) for k in range(2)]
    before = lax.broadcasted_iota(jnp.int32, (tokens, tokens), 0)
    after = lax.broadcasted_iota(jnp.int32, (tokens, tokens), 1)
    earlier = (before < after).astype(F32).astype(BF16)
    slot = jnp.dot((named[0] + named[1]).astype(BF16), earlier, preferred_element_type=F32)
    return named, slot


def tile_of(first, second, j):
    if j < 3:
        return first[:, j * LANES : (j + 1) * LANES]
    if j < 6:
        return second[:, (j - 3) * LANES : (j - 2) * LANES]
    return jnp.concatenate([first[:, 3 * LANES :], second[:, 3 * LANES :]], axis=1)


def pair_of(tiles):
    half = LANES // 2
    first = jnp.concatenate(tiles[0:3] + [tiles[6][:, :half]], axis=1)
    second = jnp.concatenate(tiles[3:6] + [tiles[6][:, half:]], axis=1)
    return first, second


def chunks(size, step):
    return [(at, min(at + step, size)) for at in range(0, size, step)]


def copies(sources, targets, semaphores):
    started = [
        pltpu.make_async_copy(source, target, semaphores.at[i])
        for i, (source, target) in enumerate(zip(sources, targets))
    ]
    for copy in started:
        copy.start()
    return started


def dispatch_kernel(
    ids_hbm,
    probs_hbm,
    tok_hbm,
    cot_hbm,
    up_hbm,
    down_hbm,
    out_ref,
    up_ref,
    down_ref,
    scratch,
    ids_ref,
    probs_ref,
    tok_ref,
    cot_ref,
    semaphores,
):
    experts = out_ref.shape[0] // BLOCK
    started = copies(
        (ids_hbm, probs_hbm, tok_hbm, cot_hbm, up_hbm, down_hbm),
        (ids_ref, probs_ref, tok_ref, cot_ref, up_ref, down_ref),
        semaphores,
    )
    for copy in started[:4]:
        copy.wait()
    named, slot = one_hots(ids_ref, experts)
    either = named[0] + named[1]
    weight = named[0] * probs_ref[0:1, :] + named[1] * probs_ref[1:2, :]
    across = (((1,), (1,)), ((), ()))
    for s in range(CAP):
        here = (slot == s).astype(F32)
        pick = (either * here).astype(BF16)
        rows = lax.dot_general(pick, tok_ref[...], across, preferred_element_type=F32)
        grads = lax.dot_general(pick, cot_ref[...], across, preferred_element_type=F32)
        grads = grads * jnp.sum(weight * here, axis=1, keepdims=True)
        for j in range(7):
            scratch[pl.ds(s * 7 + j, experts, stride=BLOCK), :] = tile_of(rows, grads, j)
    for r in range(7 * CAP, BLOCK):
        scratch[pl.ds(r, experts, stride=BLOCK), :] = jnp.zeros((experts, LANES), F32)
    out_ref[...] = scratch[...].astype(BF16)
    for copy in started[4:]:
        copy.wait()


def row_of(device, slot, each):
    return device * SHARE + (HEAD + (slot - 1) * each if slot else 0)


def up_kernel(
    block_ref, up_ref, down_ref, out_hbm, scratch, row_ref, grad_ref, out_ref, semaphores
):
    sources = block_ref.shape[0] // BLOCK
    feat, hidden = up_ref.shape
    devices = out_ref.shape[0] // SHARE
    each = sources // devices
    scratch[...] = block_ref[...].astype(F32)
    for d in range(devices):
        for s in range(CAP):
            rows = slice(row_of(d, s, each), row_of(d, s, each) + each)
            for j in range(7):
                tile = scratch[pl.ds(d * each * BLOCK + s * 7 + j, each, stride=BLOCK), :]
                if j < 3:
                    row_ref[rows, j * LANES : (j + 1) * LANES] = tile
                elif j < 6:
                    grad_ref[rows, (j - 3) * LANES : (j - 2) * LANES] = tile
                else:
                    row_ref[rows, 3 * LANES :] = tile
        pad = slice(d * SHARE + each, d * SHARE + HEAD)
        row_ref[pad, :] = jnp.zeros((HEAD - each, row_ref.shape[1]), F32)
        grad_ref[pad, :] = jnp.zeros((HEAD - each, grad_ref.shape[1]), F32)
    rows = row_ref[:, :feat].astype(BF16)
    grads = jnp.concatenate([grad_ref[...], row_ref[:, feat:]], axis=1).astype(BF16)
    started = []
    for left, weight, base in ((rows, up_ref, 0), (grads, down_ref, hidden)):
        for at, to in chunks(hidden, 512):
            span = slice(base + at, base + to)
            out_ref[:, span] = jnp.dot(
                left, weight[:, at:to], preferred_element_type=F32
            ).astype(BF16)
            started.append(
                pltpu.make_async_copy(
                    out_ref.at[:, span], out_hbm.at[:, span], semaphores.at[len(started)]
                )
            )
            started[-1].start()
    for copy in started:
        copy.wait()


def middle_kernel(sum_ref, small_ref, large_ref, scratch):
    hidden = sum_ref.shape[1] // 2
    each = small_ref.shape[0] // 2
    up_sum = sum_ref[:, :hidden].astype(F32)
    grad = sum_ref[:, hidden:].astype(F32)
    sigmoid = 1.0 / (1.0 + jnp.exp(-up_sum))
    act = (up_sum * sigmoid).astype(BF16).astype(F32)
    up_grad = grad * sigmoid * (1.0 + up_sum * (1.0 - sigmoid))
    score = jnp.sum(act * grad, axis=1, keepdims=True)
    high = score.astype(BF16).astype(F32)
    lane = lax.broadcasted_iota(jnp.int32, (sum_ref.shape[0], LANES), 1)
    score = jnp.where(lane == 0, high, jnp.where(lane == 1, score - high, 0.0))
    scratch[:each, :hidden] = act[:each]
    scratch[each:, :hidden] = up_grad[:each]
    scratch[:each, hidden:] = score[:each]
    scratch[each:, hidden:] = jnp.zeros((each, LANES), F32)
    small_ref[...] = scratch[...].astype(BF16)
    rest = slice(HEAD, HEAD + 2 * each)
    large_ref[:, :hidden] = act[rest].astype(BF16)
    large_ref[:, hidden : 2 * hidden] = up_grad[rest].astype(BF16)
    large_ref[:, 2 * hidden :] = score[rest].astype(BF16)


def columns_at(at, to):
    return (slice(None), slice(at, to))


def pack(out_ref, part_ref, scores, target, rows, devices, each, slots, height):
    for d in range(devices):
        for s in range(slots):
            low, high = rows(d, s)
            left = slice(low, low + each)
            right = slice(high, high + each)
            out, part = out_ref[left, :], part_ref[right, :]
            for j in range(7):
                target[pl.ds(d * each * height + s * 7 + j, each, stride=height), :] = tile_of(
                    out, part, j
                )
            target[pl.ds(d * each * height + 7 * slots + s, each, stride=height), :] = scores[
                left, :
            ]


def down_small_kernel(
    devices,
    join_hbm,
    up_ref,
    down_hbm,
    out_ref,
    target,
    join_ref,
    down_ref,
    out_rows,
    part_rows,
    score_rows,
    semaphores,
):
    hidden = up_ref.shape[1]
    across = (((1,), (1,)), ((), ()))
    started = copies((join_hbm, down_hbm), (join_ref, down_ref), semaphores)
    started[0].wait()
    joined = join_ref[:, :hidden]
    part_rows[...] = lax.dot_general(joined, up_ref[...], across, preferred_element_type=F32)
    score_rows[...] = join_ref[:, hidden:].astype(F32)
    started[1].wait()
    out_rows[...] = lax.dot_general(joined, down_ref[...], across, preferred_element_type=F32)
    each = join_ref.shape[0] // devices // 2
    pack(
        out_rows,
        part_rows,
        score_rows,
        target,
        lambda d, s: (2 * each * d, 2 * each * d + each),
        devices,
        each,
        1,
        SMALL,
    )
    out_ref[...] = target[...].astype(BF16)


def down_large_kernel(
    devices,
    join_hbm,
    up_ref,
    down_hbm,
    out_ref,
    target,
    join_ref,
    down_ref,
    out_rows,
    part_rows,
    score_rows,
    semaphores,
):
    hidden = up_ref.shape[1]
    across = (((1,), (1,)), ((), ()))
    spans = chunks(hidden, 1024)
    parts = [columns_at(base + at, base + to) for base in (hidden, 0) for at, to in spans]
    parts.append(columns_at(2 * hidden, 2 * hidden + LANES))
    own = [columns_at(at, to) for at, to in spans]
    count = len(spans)
    from_join = copies(
        [join_hbm.at[part] for part in parts[:count]],
        [join_ref.at[part] for part in parts[:count]],
        semaphores,
    )
    from_down = copies(
        [down_hbm.at[part] for part in own],
        [down_ref.at[part] for part in own],
        semaphores.at[pl.ds(count, count)],
    )
    started = copies(
        [join_hbm.at[part] for part in parts[count:]],
        [join_ref.at[part] for part in parts[count:]],
        semaphores.at[pl.ds(2 * count, count + 1)],
    )
    total = 0.0
    for i in range(count):
        from_join[i].wait()
        total += lax.dot_general(
            join_ref[parts[i]], up_ref[own[i]], across, preferred_element_type=F32
        )
    part_rows[...] = total
    total = 0.0
    for i in range(count):
        from_down[i].wait()
        started[i].wait()
        total += lax.dot_general(
            join_ref[parts[count + i]], down_ref[own[i]], across, preferred_element_type=F32
        )
    out_rows[...] = total
    started[-1].wait()
    score_rows[...] = join_ref[parts[-1]].astype(F32)
    each = join_ref.shape[0] // devices // 2

    def rows(d, s):
        return ((2 * d + s) * each,) * 2

    pack(
        out_rows, part_rows, score_rows, target, rows, devices, each, 2, LARGE
    )
    out_ref[...] = target[...].astype(BF16)


def combine_kernel(
    ids_ref, probs_ref, small_ref, large_ref, mixed_ref, grad_ref, score_ref, first_rows, rest_rows
):
    experts = small_ref.shape[0] // SMALL
    named, slot = one_hots(ids_ref, experts)
    first_rows[...] = small_ref[...].astype(F32)
    rest_rows[...] = large_ref[...].astype(F32)

    def came(slot, j):
        if slot == 0:
            return first_rows[pl.ds(j, experts, stride=SMALL), :]
        at = (slot - 1) * 7 + j if j < 7 else 14 + slot - 1
        return rest_rows[pl.ds(at, experts, stride=LARGE), :]

    along = (((0,), (0,)), ((), ()))
    outs, parts, picks = [], [], []
    scores = [jnp.zeros((1, ids_ref.shape[1]), F32) for _ in range(2)]
    for s in range(CAP):
        here = (slot == s).astype(F32)
        first, second = pair_of([came(s, j) for j in range(7)])
        outs.append(first)
        parts.append(second)
        picks.append(jnp.concatenate([named[0] * here, named[1] * here], axis=1))
        tail = came(s, 7)
        value = tail[:, 0:1] + tail[:, 1:2]
        for k in range(2):
            scores[k] += jnp.sum(named[k] * here * value, axis=0, keepdims=True)
    outs = jnp.concatenate(outs, axis=0).astype(BF16)
    parts = jnp.concatenate(parts, axis=0).astype(BF16)
    picks = jnp.concatenate(picks, axis=0)
    tokens = ids_ref.shape[1]
    either = (picks[:, :tokens] + picks[:, tokens:]).astype(BF16)
    got = lax.dot_general(outs, picks.astype(BF16), along, preferred_element_type=F32)
    mixed_ref[...] = (
        got[:, :tokens] * probs_ref[0:1, :] + got[:, tokens:] * probs_ref[1:2, :]
    ).astype(BF16)
    grad_ref[...] = lax.dot_general(parts, either, along, preferred_element_type=F32).astype(BF16)
    score_ref[...] = jnp.concatenate(scores, axis=0) / probs_ref[...]


def gather_by_pairs(rows, devices):
    pairs = [[i, i + 1] for i in range(0, devices, 2)]
    parities = [list(range(i, devices, 2)) for i in range(2)]
    for groups in (pairs, parities):
        rows = lax.all_gather(rows, "tensor", axis=0, tiled=True, axis_index_groups=groups)
    return rows


def in_hbm(array):
    return pltpu.with_memory_space_constraint(array, pltpu.HBM)


def exchange(block, experts):
    shape = block.shape
    block = block.reshape(experts, -1, LANES)
    block = lax.all_to_all(block, "dp", split_axis=0, concat_axis=0, tiled=True)
    return block.reshape(shape)


def per_device(tokens, cotangent, expert_ids, route_probs, up_weight, down_weight):
    count, feat = tokens.shape
    experts = lax.axis_size("dp")
    hidden = up_weight.shape[2]
    ids, probs = expert_ids.T, route_probs.T
    up, down = up_weight[0], down_weight[0].T
    packed = jax.ShapeDtypeStruct((experts * BLOCK, LANES), BF16)
    stage = [pltpu.VMEM((experts * BLOCK, LANES), F32)]
    anywhere = pl.BlockSpec(memory_space=pltpu.HBM)
    send, up_near, down_near = pl.pallas_call(
        dispatch_kernel,
        out_shape=(
            packed,
            pltpu.VMEM(up.shape, BF16),
            pltpu.VMEM(down.shape, BF16),
        ),
        in_specs=[anywhere] * 6,
        scratch_shapes=stage
        + [
            pltpu.VMEM(ids.shape, jnp.int32),
            pltpu.VMEM(probs.shape, F32),
            pltpu.VMEM((feat, count), BF16),
            pltpu.VMEM((feat, count), BF16),
            pltpu.SemaphoreType.DMA((6,)),
        ],
        compiler_params=params(14),
    )(*map(in_hbm, (ids, probs, tokens.T, cotangent.T, up, down)))
    devices = lax.axis_size("tensor")
    each = experts // devices
    partial = pl.pallas_call(
        up_kernel,
        out_shape=pltpu.HBM((devices * SHARE, 2 * hidden), BF16),
        out_specs=anywhere,
        scratch_shapes=stage
        + [
            pltpu.VMEM((devices * SHARE, 4 * LANES), F32),
            pltpu.VMEM((devices * SHARE, 3 * LANES), F32),
            pltpu.VMEM((devices * SHARE, 2 * hidden), BF16),
            pltpu.SemaphoreType.DMA((2 * len(chunks(hidden, 512)),)),
        ],
        compiler_params=params(20),
    )(exchange(send, experts), up_near, down_near)
    share = lax.psum_scatter(partial, "tensor", scatter_dimension=0, tiled=True)
    small, large = pl.pallas_call(
        middle_kernel,
        out_shape=(
            jax.ShapeDtypeStruct((2 * each, hidden + LANES), BF16),
            jax.ShapeDtypeStruct((2 * each, 2 * hidden + LANES), BF16),
        ),
        scratch_shapes=[pltpu.VMEM((2 * each, hidden + LANES), F32)],
        compiler_params=params(14),
    )(share)
    whole = pl.BlockSpec(memory_space=pltpu.VMEM)
    joined = lax.all_gather(large, "tensor", axis=0, tiled=True)
    joined_small = gather_by_pairs(small, devices)
    products = [
        pltpu.VMEM((2 * each * devices, feat), F32),
        pltpu.VMEM((2 * each * devices, feat), F32),
        pltpu.VMEM((2 * each * devices, LANES), F32),
    ]
    back_small = pl.pallas_call(
        functools.partial(down_small_kernel, devices),
        out_shape=jax.ShapeDtypeStruct((experts * SMALL, LANES), BF16),
        in_specs=[anywhere, whole, anywhere],
        scratch_shapes=[
            pltpu.VMEM((experts * SMALL, LANES), F32),
            pltpu.VMEM(joined_small.shape, BF16),
            pltpu.VMEM(down.shape, BF16),
        ]
        + products
        + [pltpu.SemaphoreType.DMA((2,))],
        compiler_params=params(20),
    )(in_hbm(joined_small), up_near, in_hbm(down))
    back_small = exchange(back_small, experts)
    back = pl.pallas_call(
        functools.partial(down_large_kernel, devices),
        out_shape=jax.ShapeDtypeStruct((experts * LARGE, LANES), BF16),
        in_specs=[anywhere, whole, anywhere],
        scratch_shapes=[
            pltpu.VMEM((experts * LARGE, LANES), F32),
            pltpu.VMEM(joined.shape, BF16),
            pltpu.VMEM(down.shape, BF16),
        ]
        + products
        + [pltpu.SemaphoreType.DMA((3 * len(chunks(hidden, 1024)) + 1,))],
        compiler_params=params(20),
    )(in_hbm(joined), up_near, in_hbm(down))
    mixed, input_grad, prob_grad = pl.pallas_call(
        combine_kernel,
        out_shape=(
            jax.ShapeDtypeStruct((feat, count), BF16),
            jax.ShapeDtypeStruct((feat, count), BF16),
            jax.ShapeDtypeStruct((2, count), F32),
        ),
        scratch_shapes=[
            pltpu.VMEM((experts * SMALL, LANES), F32),
            pltpu.VMEM((experts * LARGE, LANES), F32),
        ],
        compiler_params=params(14),
    )(ids, probs, back_small, exchange(back, experts))
    return mixed.T, input_grad.T, prob_grad.T


def solution(mesh):
    return jax.shard_map(
        per_device,
        mesh=mesh,
        in_specs=(
            P("dp", "tensor"),
            P("dp", "tensor"),
            P("dp", None),
            P("dp", None),
            P("dp", "tensor", None),
            P("dp", None, "tensor"),
        ),
        out_specs=(P("dp", "tensor"), P("dp", "tensor"), P("dp", None)),
        check_vma=False,
    )
```

```python
import functools

import jax
import jax.numpy as jnp
from jax import lax
from jax.experimental import pallas as pl
from jax.experimental.pallas import tpu as pltpu
from jax.sharding import PartitionSpec as P

CAP = 3
LANES = 128
BLOCK = 24
SHARE = 40
HEAD = 16
SMALL = 8
LARGE = 16
F32 = jnp.float32
BF16 = jnp.bfloat16
MIB = 1024 * 1024


def params(mib):
    return pltpu.CompilerParams(vmem_limit_bytes=mib * MIB)


def one_hots(ids_ref, experts):
    tokens = ids_ref.shape[1]
    expert = lax.broadcasted_iota(jnp.int32, (experts, tokens), 0)
    named = [(ids_ref[k : k + 1, :] == expert).astype(F32) for k in range(2)]
    before = lax.broadcasted_iota(jnp.int32, (tokens, tokens), 0)
    after = lax.broadcasted_iota(jnp.int32, (tokens, tokens), 1)
    earlier = (before < after).astype(F32).astype(BF16)
    slot = jnp.dot((named[0] + named[1]).astype(BF16), earlier, preferred_element_type=F32)
    return named, slot


def tile_of(first, second, j):
    if j < 3:
        return first[:, j * LANES : (j + 1) * LANES]
    if j < 6:
        return second[:, (j - 3) * LANES : (j - 2) * LANES]
    return jnp.concatenate([first[:, 3 * LANES :], second[:, 3 * LANES :]], axis=1)


def pair_of(tiles):
    half = LANES // 2
    first = jnp.concatenate(tiles[0:3] + [tiles[6][:, :half]], axis=1)
    second = jnp.concatenate(tiles[3:6] + [tiles[6][:, half:]], axis=1)
    return first, second


def chunks(size, step):
    return [(at, min(at + step, size)) for at in range(0, size, step)]


def copies(sources, targets, semaphores):
    started = [
        pltpu.make_async_copy(source, target, semaphores.at[i])
        for i, (source, target) in enumerate(zip(sources, targets))
    ]
    for copy in started:
        copy.start()
    return started


def dispatch_kernel(
    ids_hbm,
    probs_hbm,
    tok_hbm,
    cot_hbm,
    _up,
    _down,
    out_ref,
    scratch,
    ids_ref,
    probs_ref,
    tok_ref,
    cot_ref,
    semaphores,
):
    experts = out_ref.shape[0] // BLOCK
    started = copies(
        (ids_hbm, probs_hbm, tok_hbm, cot_hbm),
        (ids_ref, probs_ref, tok_ref, cot_ref),
        semaphores,
    )
    for copy in started:
        copy.wait()
    named, slot = one_hots(ids_ref, experts)
    either = named[0] + named[1]
    weight = named[0] * probs_ref[0:1, :] + named[1] * probs_ref[1:2, :]
    across = (((1,), (1,)), ((), ()))
    for s in range(CAP):
        here = (slot == s).astype(F32)
        pick = (either * here).astype(BF16)
        rows = lax.dot_general(pick, tok_ref[...], across, preferred_element_type=F32)
        grads = lax.dot_general(pick, cot_ref[...], across, preferred_element_type=F32)
        grads = grads * jnp.sum(weight * here, axis=1, keepdims=True)
        for j in range(7):
            scratch[pl.ds(s * 7 + j, experts, stride=BLOCK), :] = tile_of(rows, grads, j)
    for r in range(7 * CAP, BLOCK):
        scratch[pl.ds(r, experts, stride=BLOCK), :] = jnp.zeros((experts, LANES), F32)
    out_ref[...] = scratch[...].astype(BF16)


def row_of(device, slot, each):
    return device * SHARE + (HEAD + (slot - 1) * each if slot else 0)


def up_kernel(
    block_ref, up_ref, down_ref, out_hbm, scratch, row_ref, grad_ref, out_ref, semaphores
):
    sources = block_ref.shape[0] // BLOCK
    feat, hidden = up_ref.shape
    devices = out_ref.shape[0] // SHARE
    each = sources // devices
    scratch[...] = block_ref[...].astype(F32)
    for d in range(devices):
        for s in range(CAP):
            rows = slice(row_of(d, s, each), row_of(d, s, each) + each)
            for j in range(7):
                tile = scratch[pl.ds(d * each * BLOCK + s * 7 + j, each, stride=BLOCK), :]
                if j < 3:
                    row_ref[rows, j * LANES : (j + 1) * LANES] = tile
                elif j < 6:
                    grad_ref[rows, (j - 3) * LANES : (j - 2) * LANES] = tile
                else:
                    row_ref[rows, 3 * LANES :] = tile
        pad = slice(d * SHARE + each, d * SHARE + HEAD)
        row_ref[pad, :] = jnp.zeros((HEAD - each, row_ref.shape[1]), F32)
        grad_ref[pad, :] = jnp.zeros((HEAD - each, grad_ref.shape[1]), F32)
    rows = row_ref[:, :feat].astype(BF16)
    grads = jnp.concatenate([grad_ref[...], row_ref[:, feat:]], axis=1).astype(BF16)
    started = []
    for left, weight, base in ((rows, up_ref, 0), (grads, down_ref, hidden)):
        for at, to in chunks(hidden, 512):
            span = slice(base + at, base + to)
            out_ref[:, span] = jnp.dot(
                left, weight[:, at:to], preferred_element_type=F32
            ).astype(BF16)
            started.append(
                pltpu.make_async_copy(
                    out_ref.at[:, span], out_hbm.at[:, span], semaphores.at[len(started)]
                )
            )
            started[-1].start()
    for copy in started:
        copy.wait()


def middle_kernel(sum_ref, small_ref, large_ref, scratch):
    hidden = sum_ref.shape[1] // 2
    each = small_ref.shape[0] // 2
    up_sum = sum_ref[:, :hidden].astype(F32)
    grad = sum_ref[:, hidden:].astype(F32)
    sigmoid = 1.0 / (1.0 + jnp.exp(-up_sum))
    act = (up_sum * sigmoid).astype(BF16).astype(F32)
    up_grad = grad * sigmoid * (1.0 + up_sum * (1.0 - sigmoid))
    score = jnp.sum(act * grad, axis=1, keepdims=True)
    high = score.astype(BF16).astype(F32)
    lane = lax.broadcasted_iota(jnp.int32, (sum_ref.shape[0], LANES), 1)
    score = jnp.where(lane == 0, high, jnp.where(lane == 1, score - high, 0.0))
    scratch[:each, :hidden] = act[:each]
    scratch[each:, :hidden] = up_grad[:each]
    scratch[:each, hidden:] = score[:each]
    scratch[each:, hidden:] = jnp.zeros((each, LANES), F32)
    small_ref[...] = scratch[...].astype(BF16)
    rest = slice(HEAD, HEAD + 2 * each)
    large_ref[:, :hidden] = act[rest].astype(BF16)
    large_ref[:, hidden : 2 * hidden] = up_grad[rest].astype(BF16)
    large_ref[:, 2 * hidden :] = score[rest].astype(BF16)


def columns_at(at, to):
    return (slice(None), slice(at, to))


def pack(out_ref, part_ref, scores, target, rows, devices, each, slots, height):
    for d in range(devices):
        for s in range(slots):
            low, high = rows(d, s)
            left = slice(low, low + each)
            right = slice(high, high + each)
            out, part = out_ref[left, :], part_ref[right, :]
            for j in range(7):
                target[pl.ds(d * each * height + s * 7 + j, each, stride=height), :] = tile_of(
                    out, part, j
                )
            target[pl.ds(d * each * height + 7 * slots + s, each, stride=height), :] = scores[
                left, :
            ]


def down_small_kernel(
    devices,
    join_hbm,
    up_ref,
    down_hbm,
    out_ref,
    target,
    join_ref,
    down_ref,
    out_rows,
    part_rows,
    score_rows,
    semaphores,
):
    hidden = up_ref.shape[1]
    across = (((1,), (1,)), ((), ()))
    spans = chunks(hidden, 1024)
    own = [columns_at(at, to) for at, to in spans]
    parts = own[:-1] + [columns_at(spans[-1][0], hidden + LANES)]
    count = len(spans)
    from_join = copies(
        [join_hbm.at[part] for part in parts], [join_ref.at[part] for part in parts], semaphores
    )
    from_down = copies(
        [down_hbm.at[part] for part in own],
        [down_ref.at[part] for part in own],
        semaphores.at[pl.ds(count, count)],
    )
    total = 0.0
    for i in range(count):
        from_join[i].wait()
        total += lax.dot_general(
            join_ref[own[i]], up_ref[own[i]], across, preferred_element_type=F32
        )
    part_rows[...] = total
    score_rows[...] = join_ref[:, hidden:].astype(F32)
    total = 0.0
    for i in range(count):
        from_down[i].wait()
        total += lax.dot_general(
            join_ref[own[i]], down_ref[own[i]], across, preferred_element_type=F32
        )
    out_rows[...] = total
    each = join_ref.shape[0] // devices // 2
    pack(
        out_rows,
        part_rows,
        score_rows,
        target,
        lambda d, s: (2 * each * d, 2 * each * d + each),
        devices,
        each,
        1,
        SMALL,
    )
    out_ref[...] = target[...].astype(BF16)


def down_large_kernel(
    devices,
    join_hbm,
    up_ref,
    down_hbm,
    out_ref,
    target,
    join_ref,
    down_ref,
    out_rows,
    part_rows,
    score_rows,
    semaphores,
):
    hidden = up_ref.shape[1]
    across = (((1,), (1,)), ((), ()))
    spans = chunks(hidden, 1024)
    parts = [columns_at(base + at, base + to) for base in (hidden, 0) for at, to in spans]
    parts.append(columns_at(2 * hidden, 2 * hidden + LANES))
    own = [columns_at(at, to) for at, to in spans]
    count = len(spans)
    from_join = copies(
        [join_hbm.at[part] for part in parts[:count]],
        [join_ref.at[part] for part in parts[:count]],
        semaphores,
    )
    from_down = copies(
        [down_hbm.at[part] for part in own],
        [down_ref.at[part] for part in own],
        semaphores.at[pl.ds(count, count)],
    )
    started = copies(
        [join_hbm.at[part] for part in parts[count:]],
        [join_ref.at[part] for part in parts[count:]],
        semaphores.at[pl.ds(2 * count, count + 1)],
    )
    total = 0.0
    for i in range(count):
        from_join[i].wait()
        total += lax.dot_general(
            join_ref[parts[i]], up_ref[own[i]], across, preferred_element_type=F32
        )
    part_rows[...] = total
    total = 0.0
    for i in range(count):
        from_down[i].wait()
        started[i].wait()
        total += lax.dot_general(
            join_ref[parts[count + i]], down_ref[own[i]], across, preferred_element_type=F32
        )
    out_rows[...] = total
    started[-1].wait()
    score_rows[...] = join_ref[parts[-1]].astype(F32)
    each = join_ref.shape[0] // devices // 2

    def rows(d, s):
        return ((2 * d + s) * each,) * 2

    pack(
        out_rows, part_rows, score_rows, target, rows, devices, each, 2, LARGE
    )
    out_ref[...] = target[...].astype(BF16)


def combine_kernel(
    ids_ref, probs_ref, small_ref, large_ref, mixed_ref, grad_ref, score_ref, first_rows, rest_rows
):
    experts = small_ref.shape[0] // SMALL
    named, slot = one_hots(ids_ref, experts)
    first_rows[...] = small_ref[...].astype(F32)
    rest_rows[...] = large_ref[...].astype(F32)

    def came(slot, j):
        if slot == 0:
            return first_rows[pl.ds(j, experts, stride=SMALL), :]
        at = (slot - 1) * 7 + j if j < 7 else 14 + slot - 1
        return rest_rows[pl.ds(at, experts, stride=LARGE), :]

    along = (((0,), (0,)), ((), ()))
    outs, parts, picks = [], [], []
    scores = [jnp.zeros((1, ids_ref.shape[1]), F32) for _ in range(2)]
    for s in range(CAP):
        here = (slot == s).astype(F32)
        first, second = pair_of([came(s, j) for j in range(7)])
        outs.append(first)
        parts.append(second)
        picks.append(jnp.concatenate([named[0] * here, named[1] * here], axis=1))
        tail = came(s, 7)
        value = tail[:, 0:1] + tail[:, 1:2]
        for k in range(2):
            scores[k] += jnp.sum(named[k] * here * value, axis=0, keepdims=True)
    outs = jnp.concatenate(outs, axis=0).astype(BF16)
    parts = jnp.concatenate(parts, axis=0).astype(BF16)
    picks = jnp.concatenate(picks, axis=0)
    tokens = ids_ref.shape[1]
    either = (picks[:, :tokens] + picks[:, tokens:]).astype(BF16)
    got = lax.dot_general(outs, picks.astype(BF16), along, preferred_element_type=F32)
    mixed_ref[...] = (
        got[:, :tokens] * probs_ref[0:1, :] + got[:, tokens:] * probs_ref[1:2, :]
    ).astype(BF16)
    grad_ref[...] = lax.dot_general(parts, either, along, preferred_element_type=F32).astype(BF16)
    score_ref[...] = jnp.concatenate(scores, axis=0) / probs_ref[...]


def in_vmem(array):
    return pltpu.with_memory_space_constraint(array, pltpu.VMEM)


def in_hbm(array):
    return pltpu.with_memory_space_constraint(array, pltpu.HBM)


def exchange(block, experts):
    shape = block.shape
    block = block.reshape(experts, -1, LANES)
    block = lax.all_to_all(block, "dp", split_axis=0, concat_axis=0, tiled=True)
    return block.reshape(shape)


def per_device(tokens, cotangent, expert_ids, route_probs, up_weight, down_weight):
    count, feat = tokens.shape
    experts = lax.axis_size("dp")
    hidden = up_weight.shape[2]
    ids, probs = expert_ids.T, route_probs.T
    up, down = up_weight[0], down_weight[0].T
    packed = jax.ShapeDtypeStruct((experts * BLOCK, LANES), BF16)
    stage = [pltpu.VMEM((experts * BLOCK, LANES), F32)]
    anywhere = pl.BlockSpec(memory_space=pltpu.HBM)
    send = pl.pallas_call(
        dispatch_kernel,
        out_shape=packed,
        in_specs=[anywhere] * 6,
        scratch_shapes=stage
        + [
            pltpu.VMEM(ids.shape, jnp.int32),
            pltpu.VMEM(probs.shape, F32),
            pltpu.VMEM((feat, count), BF16),
            pltpu.VMEM((feat, count), BF16),
            pltpu.SemaphoreType.DMA((4,)),
        ],
        compiler_params=params(14),
    )(*map(in_hbm, (ids, probs, tokens.T, cotangent.T, up, down)))
    devices = lax.axis_size("tensor")
    each = experts // devices
    partial = pl.pallas_call(
        up_kernel,
        out_shape=pltpu.HBM((devices * SHARE, 2 * hidden), BF16),
        out_specs=anywhere,
        scratch_shapes=stage
        + [
            pltpu.VMEM((devices * SHARE, 4 * LANES), F32),
            pltpu.VMEM((devices * SHARE, 3 * LANES), F32),
            pltpu.VMEM((devices * SHARE, 2 * hidden), BF16),
            pltpu.SemaphoreType.DMA((2 * len(chunks(hidden, 512)),)),
        ],
        compiler_params=params(20),
    )(exchange(send, experts), in_vmem(up), in_vmem(down))
    share = lax.psum_scatter(partial, "tensor", scatter_dimension=0, tiled=True)
    small, large = pl.pallas_call(
        middle_kernel,
        out_shape=(
            jax.ShapeDtypeStruct((2 * each, hidden + LANES), BF16),
            jax.ShapeDtypeStruct((2 * each, 2 * hidden + LANES), BF16),
        ),
        scratch_shapes=[pltpu.VMEM((2 * each, hidden + LANES), F32)],
        compiler_params=params(14),
    )(share)
    whole = pl.BlockSpec(memory_space=pltpu.VMEM)
    joined = lax.all_gather(large, "tensor", axis=0, tiled=True)
    joined_small = lax.all_gather(small, "tensor", axis=0, tiled=True)
    products = [
        pltpu.VMEM((2 * each * devices, feat), F32),
        pltpu.VMEM((2 * each * devices, feat), F32),
        pltpu.VMEM((2 * each * devices, LANES), F32),
    ]
    back_small = pl.pallas_call(
        functools.partial(down_small_kernel, devices),
        out_shape=jax.ShapeDtypeStruct((experts * SMALL, LANES), BF16),
        in_specs=[anywhere, whole, anywhere],
        scratch_shapes=[
            pltpu.VMEM((experts * SMALL, LANES), F32),
            pltpu.VMEM(joined_small.shape, BF16),
            pltpu.VMEM(down.shape, BF16),
        ]
        + products
        + [pltpu.SemaphoreType.DMA((2 * len(chunks(hidden, 1024)),))],
        compiler_params=params(20),
    )(in_hbm(joined_small), up, in_hbm(down))
    back_small = exchange(back_small, experts)
    back = pl.pallas_call(
        functools.partial(down_large_kernel, devices),
        out_shape=jax.ShapeDtypeStruct((experts * LARGE, LANES), BF16),
        in_specs=[anywhere, whole, anywhere],
        scratch_shapes=[
            pltpu.VMEM((experts * LARGE, LANES), F32),
            pltpu.VMEM(joined.shape, BF16),
            pltpu.VMEM(down.shape, BF16),
        ]
        + products
        + [pltpu.SemaphoreType.DMA((3 * len(chunks(hidden, 1024)) + 1,))],
        compiler_params=params(20),
    )(in_hbm(joined), up, in_hbm(down))
    mixed, input_grad, prob_grad = pl.pallas_call(
        combine_kernel,
        out_shape=(
            jax.ShapeDtypeStruct((feat, count), BF16),
            jax.ShapeDtypeStruct((feat, count), BF16),
            jax.ShapeDtypeStruct((2, count), F32),
        ),
        scratch_shapes=[
            pltpu.VMEM((experts * SMALL, LANES), F32),
            pltpu.VMEM((experts * LARGE, LANES), F32),
        ],
        compiler_params=params(14),
    )(ids, probs, back_small, exchange(back, experts))
    return mixed.T, input_grad.T, prob_grad.T


def solution(mesh):
    return jax.shard_map(
        per_device,
        mesh=mesh,
        in_specs=(
            P("dp", "tensor"),
            P("dp", "tensor"),
            P("dp", None),
            P("dp", None),
            P("dp", "tensor", None),
            P("dp", None, "tensor"),
        ),
        out_specs=(P("dp", "tensor"), P("dp", "tensor"), P("dp", None)),
        check_vma=False,
    )
```

```python
import functools

import jax
import jax.numpy as jnp
from jax import lax
from jax.experimental import pallas as pl
from jax.experimental.pallas import tpu as pltpu
from jax.sharding import PartitionSpec as P

CAP = 3
LANES = 128
BLOCK = 24
SHARE = 40
HEAD = 16
SMALL = 8
F32 = jnp.float32
BF16 = jnp.bfloat16
MIB = 1024 * 1024


def params(mib):
    return pltpu.CompilerParams(vmem_limit_bytes=mib * MIB)


def one_hots(ids_ref, experts):
    tokens = ids_ref.shape[1]
    expert = lax.broadcasted_iota(jnp.int32, (experts, tokens), 0)
    named = [(ids_ref[k : k + 1, :] == expert).astype(F32) for k in range(2)]
    before = lax.broadcasted_iota(jnp.int32, (tokens, tokens), 0)
    after = lax.broadcasted_iota(jnp.int32, (tokens, tokens), 1)
    earlier = (before < after).astype(F32).astype(BF16)
    slot = jnp.dot((named[0] + named[1]).astype(BF16), earlier, preferred_element_type=F32)
    return named, slot


def tile_of(first, second, j):
    if j < 3:
        return first[:, j * LANES : (j + 1) * LANES]
    if j < 6:
        return second[:, (j - 3) * LANES : (j - 2) * LANES]
    return jnp.concatenate([first[:, 3 * LANES :], second[:, 3 * LANES :]], axis=1)


def pair_of(tiles):
    half = LANES // 2
    first = jnp.concatenate(tiles[0:3] + [tiles[6][:, :half]], axis=1)
    second = jnp.concatenate(tiles[3:6] + [tiles[6][:, half:]], axis=1)
    return first, second


def chunks(size, step):
    return [(at, min(at + step, size)) for at in range(0, size, step)]


def copies(sources, targets, semaphores):
    started = [
        pltpu.make_async_copy(source, target, semaphores.at[i])
        for i, (source, target) in enumerate(zip(sources, targets))
    ]
    for copy in started:
        copy.start()
    return started


def dispatch_kernel(
    ids_hbm,
    probs_hbm,
    tok_hbm,
    cot_hbm,
    _up,
    _down,
    out_ref,
    scratch,
    ids_ref,
    probs_ref,
    tok_ref,
    cot_ref,
    semaphores,
):
    experts = out_ref.shape[0] // BLOCK
    started = copies(
        (ids_hbm, probs_hbm, tok_hbm, cot_hbm),
        (ids_ref, probs_ref, tok_ref, cot_ref),
        semaphores,
    )
    for copy in started:
        copy.wait()
    named, slot = one_hots(ids_ref, experts)
    either = named[0] + named[1]
    weight = named[0] * probs_ref[0:1, :] + named[1] * probs_ref[1:2, :]
    across = (((1,), (1,)), ((), ()))
    for s in range(CAP):
        here = (slot == s).astype(F32)
        pick = (either * here).astype(BF16)
        rows = lax.dot_general(pick, tok_ref[...], across, preferred_element_type=F32)
        grads = lax.dot_general(pick, cot_ref[...], across, preferred_element_type=F32)
        grads = grads * jnp.sum(weight * here, axis=1, keepdims=True)
        for j in range(7):
            scratch[pl.ds(s * 7 + j, experts, stride=BLOCK), :] = tile_of(rows, grads, j)
    for r in range(7 * CAP, BLOCK):
        scratch[pl.ds(r, experts, stride=BLOCK), :] = jnp.zeros((experts, LANES), F32)
    out_ref[...] = scratch[...].astype(BF16)


def row_of(device, slot, each):
    return device * SHARE + (HEAD + (slot - 1) * each if slot else 0)


def up_kernel(
    block_ref, up_ref, down_ref, out_hbm, scratch, row_ref, grad_ref, out_ref, semaphores
):
    sources = block_ref.shape[0] // BLOCK
    feat, hidden = up_ref.shape
    devices = out_ref.shape[0] // SHARE
    each = sources // devices
    scratch[...] = block_ref[...].astype(F32)
    for d in range(devices):
        for s in range(CAP):
            rows = slice(row_of(d, s, each), row_of(d, s, each) + each)
            for j in range(7):
                tile = scratch[pl.ds(d * each * BLOCK + s * 7 + j, each, stride=BLOCK), :]
                if j < 3:
                    row_ref[rows, j * LANES : (j + 1) * LANES] = tile
                elif j < 6:
                    grad_ref[rows, (j - 3) * LANES : (j - 2) * LANES] = tile
                else:
                    row_ref[rows, 3 * LANES :] = tile
        pad = slice(d * SHARE + each, d * SHARE + HEAD)
        row_ref[pad, :] = jnp.zeros((HEAD - each, row_ref.shape[1]), F32)
        grad_ref[pad, :] = jnp.zeros((HEAD - each, grad_ref.shape[1]), F32)
    rows = row_ref[:, :feat].astype(BF16)
    grads = jnp.concatenate([grad_ref[...], row_ref[:, feat:]], axis=1).astype(BF16)
    started = []
    for left, weight, base in ((rows, up_ref, 0), (grads, down_ref, hidden)):
        for at, to in chunks(hidden, 512):
            span = slice(base + at, base + to)
            out_ref[:, span] = jnp.dot(
                left, weight[:, at:to], preferred_element_type=F32
            ).astype(BF16)
            started.append(
                pltpu.make_async_copy(
                    out_ref.at[:, span], out_hbm.at[:, span], semaphores.at[len(started)]
                )
            )
            started[-1].start()
    for copy in started:
        copy.wait()


def middle_kernel(sum_ref, small_ref, large_ref, scratch):
    hidden = sum_ref.shape[1] // 2
    each = small_ref.shape[0] // 2
    up_sum = sum_ref[:, :hidden].astype(F32)
    grad = sum_ref[:, hidden:].astype(F32)
    sigmoid = 1.0 / (1.0 + jnp.exp(-up_sum))
    act = (up_sum * sigmoid).astype(BF16).astype(F32)
    up_grad = grad * sigmoid * (1.0 + up_sum * (1.0 - sigmoid))
    score = jnp.sum(act * grad, axis=1, keepdims=True)
    high = score.astype(BF16).astype(F32)
    lane = lax.broadcasted_iota(jnp.int32, (sum_ref.shape[0], LANES), 1)
    score = jnp.where(lane == 0, high, jnp.where(lane == 1, score - high, 0.0))
    scratch[:each, :hidden] = act[:each]
    scratch[each:, :hidden] = up_grad[:each]
    scratch[:each, hidden:] = score[:each]
    scratch[each:, hidden:] = jnp.zeros((each, LANES), F32)
    small_ref[...] = scratch[...].astype(BF16)
    rest = slice(HEAD, HEAD + 2 * each)
    large_ref[:, :hidden] = act[rest].astype(BF16)
    large_ref[:, hidden : 2 * hidden] = up_grad[rest].astype(BF16)
    large_ref[:, 2 * hidden :] = score[rest].astype(BF16)


def columns_at(at, to):
    return (slice(None), slice(at, to))


def place(slot, j):
    return slot * 7 + j if j < 7 else 7 * CAP + slot


def pack(out_ref, part_ref, scores, target, rows, devices, each, slots, place, height):
    for d in range(devices):
        for s in range(slots):
            low, high = rows(d, s)
            left = slice(low, low + each)
            right = slice(high, high + each)
            out, part = out_ref[left, :], part_ref[right, :]
            for j in range(7):
                at = d * each * height + place(s, j)
                target[pl.ds(at, each, stride=height), :] = tile_of(out, part, j)
            at = d * each * height + place(s, 7)
            target[pl.ds(at, each, stride=height), :] = scores[left, :]


def down_small_kernel(
    devices,
    join_hbm,
    up_ref,
    down_hbm,
    out_ref,
    target,
    join_ref,
    down_ref,
    out_rows,
    part_rows,
    score_rows,
    semaphores,
):
    hidden = up_ref.shape[1]
    across = (((1,), (1,)), ((), ()))
    spans = chunks(hidden, 1024)
    own = [columns_at(at, to) for at, to in spans]
    parts = own[:-1] + [columns_at(spans[-1][0], hidden + LANES)]
    count = len(spans)
    from_join = copies(
        [join_hbm.at[part] for part in parts], [join_ref.at[part] for part in parts], semaphores
    )
    from_down = copies(
        [down_hbm.at[part] for part in own],
        [down_ref.at[part] for part in own],
        semaphores.at[pl.ds(count, count)],
    )
    total = 0.0
    for i in range(count):
        from_join[i].wait()
        total += lax.dot_general(
            join_ref[own[i]], up_ref[own[i]], across, preferred_element_type=F32
        )
    part_rows[...] = total
    score_rows[...] = join_ref[:, hidden:].astype(F32)
    total = 0.0
    for i in range(count):
        from_down[i].wait()
        total += lax.dot_general(
            join_ref[own[i]], down_ref[own[i]], across, preferred_element_type=F32
        )
    out_rows[...] = total
    each = join_ref.shape[0] // devices // 2
    pack(
        out_rows,
        part_rows,
        score_rows,
        target,
        lambda d, s: (2 * each * d, 2 * each * d + each),
        devices,
        each,
        1,
        lambda s, j: j,
        SMALL,
    )
    out_ref[...] = target[...].astype(BF16)


def down_large_kernel(
    devices,
    join_hbm,
    up_ref,
    down_hbm,
    small_ref,
    out_ref,
    target,
    small_rows,
    join_ref,
    down_ref,
    out_rows,
    part_rows,
    score_rows,
    semaphores,
):
    hidden = up_ref.shape[1]
    across = (((1,), (1,)), ((), ()))
    spans = chunks(hidden, 1024)
    parts = [columns_at(base + at, base + to) for base in (hidden, 0) for at, to in spans]
    parts.append(columns_at(2 * hidden, 2 * hidden + LANES))
    own = [columns_at(at, to) for at, to in spans]
    count = len(spans)
    from_join = copies(
        [join_hbm.at[part] for part in parts[:count]],
        [join_ref.at[part] for part in parts[:count]],
        semaphores,
    )
    from_down = copies(
        [down_hbm.at[part] for part in own],
        [down_ref.at[part] for part in own],
        semaphores.at[pl.ds(count, count)],
    )
    started = copies(
        [join_hbm.at[part] for part in parts[count:]],
        [join_ref.at[part] for part in parts[count:]],
        semaphores.at[pl.ds(2 * count, count + 1)],
    )
    total = 0.0
    for i in range(count):
        from_join[i].wait()
        total += lax.dot_general(
            join_ref[parts[i]], up_ref[own[i]], across, preferred_element_type=F32
        )
    part_rows[...] = total
    total = 0.0
    for i in range(count):
        from_down[i].wait()
        started[i].wait()
        total += lax.dot_general(
            join_ref[parts[count + i]], down_ref[own[i]], across, preferred_element_type=F32
        )
    out_rows[...] = total
    started[-1].wait()
    score_rows[...] = join_ref[parts[-1]].astype(F32)
    each = join_ref.shape[0] // devices // 2

    def rows(d, s):
        return ((2 * d + s) * each,) * 2

    sources = small_ref.shape[0] // SMALL
    small_rows[...] = small_ref[...].astype(F32)
    for j in range(SMALL):
        target[pl.ds(place(0, j), sources, stride=BLOCK), :] = small_rows[
            pl.ds(j, sources, stride=SMALL), :
        ]
    pack(
        out_rows,
        part_rows,
        score_rows,
        target,
        rows,
        devices,
        each,
        2,
        lambda s, j: place(s + 1, j),
        BLOCK,
    )
    out_ref[...] = target[...].astype(BF16)


def combine_kernel(ids_ref, probs_ref, block_ref, mixed_ref, grad_ref, score_ref, scratch):
    experts = block_ref.shape[0] // BLOCK
    named, slot = one_hots(ids_ref, experts)
    scratch[...] = block_ref[...].astype(F32)
    along = (((0,), (0,)), ((), ()))
    outs, parts, picks = [], [], []
    scores = [jnp.zeros((1, ids_ref.shape[1]), F32) for _ in range(2)]
    for s in range(CAP):
        here = (slot == s).astype(F32)
        tiles = [scratch[pl.ds(s * 7 + j, experts, stride=BLOCK), :] for j in range(7)]
        first, second = pair_of(tiles)
        outs.append(first)
        parts.append(second)
        picks.append(jnp.concatenate([named[0] * here, named[1] * here], axis=1))
        tail = scratch[pl.ds(7 * CAP + s, experts, stride=BLOCK), :]
        value = tail[:, 0:1] + tail[:, 1:2]
        for k in range(2):
            scores[k] += jnp.sum(named[k] * here * value, axis=0, keepdims=True)
    outs = jnp.concatenate(outs, axis=0).astype(BF16)
    parts = jnp.concatenate(parts, axis=0).astype(BF16)
    picks = jnp.concatenate(picks, axis=0)
    tokens = ids_ref.shape[1]
    either = (picks[:, :tokens] + picks[:, tokens:]).astype(BF16)
    got = lax.dot_general(outs, picks.astype(BF16), along, preferred_element_type=F32)
    mixed_ref[...] = (
        got[:, :tokens] * probs_ref[0:1, :] + got[:, tokens:] * probs_ref[1:2, :]
    ).astype(BF16)
    grad_ref[...] = lax.dot_general(parts, either, along, preferred_element_type=F32).astype(BF16)
    score_ref[...] = jnp.concatenate(scores, axis=0) / probs_ref[...]


def in_vmem(array):
    return pltpu.with_memory_space_constraint(array, pltpu.VMEM)


def in_hbm(array):
    return pltpu.with_memory_space_constraint(array, pltpu.HBM)


def exchange(block, experts):
    shape = block.shape
    block = block.reshape(experts, -1, LANES)
    block = lax.all_to_all(block, "dp", split_axis=0, concat_axis=0, tiled=True)
    return block.reshape(shape)


def per_device(tokens, cotangent, expert_ids, route_probs, up_weight, down_weight):
    count, feat = tokens.shape
    experts = lax.axis_size("dp")
    hidden = up_weight.shape[2]
    ids, probs = expert_ids.T, route_probs.T
    up, down = up_weight[0], down_weight[0].T
    packed = jax.ShapeDtypeStruct((experts * BLOCK, LANES), BF16)
    stage = [pltpu.VMEM((experts * BLOCK, LANES), F32)]
    anywhere = pl.BlockSpec(memory_space=pltpu.HBM)
    send = pl.pallas_call(
        dispatch_kernel,
        out_shape=packed,
        in_specs=[anywhere] * 6,
        scratch_shapes=stage
        + [
            pltpu.VMEM(ids.shape, jnp.int32),
            pltpu.VMEM(probs.shape, F32),
            pltpu.VMEM((feat, count), BF16),
            pltpu.VMEM((feat, count), BF16),
            pltpu.SemaphoreType.DMA((4,)),
        ],
        compiler_params=params(14),
    )(*map(in_hbm, (ids, probs, tokens.T, cotangent.T, up, down)))
    devices = lax.axis_size("tensor")
    each = experts // devices
    partial = pl.pallas_call(
        up_kernel,
        out_shape=pltpu.HBM((devices * SHARE, 2 * hidden), BF16),
        out_specs=anywhere,
        scratch_shapes=stage
        + [
            pltpu.VMEM((devices * SHARE, 4 * LANES), F32),
            pltpu.VMEM((devices * SHARE, 3 * LANES), F32),
            pltpu.VMEM((devices * SHARE, 2 * hidden), BF16),
            pltpu.SemaphoreType.DMA((2 * len(chunks(hidden, 512)),)),
        ],
        compiler_params=params(20),
    )(exchange(send, experts), in_vmem(up), in_vmem(down))
    share = lax.psum_scatter(partial, "tensor", scatter_dimension=0, tiled=True)
    small, large = pl.pallas_call(
        middle_kernel,
        out_shape=(
            jax.ShapeDtypeStruct((2 * each, hidden + LANES), BF16),
            jax.ShapeDtypeStruct((2 * each, 2 * hidden + LANES), BF16),
        ),
        scratch_shapes=[pltpu.VMEM((2 * each, hidden + LANES), F32)],
        compiler_params=params(14),
    )(share)
    whole = pl.BlockSpec(memory_space=pltpu.VMEM)
    joined = lax.all_gather(large, "tensor", axis=0, tiled=True)
    joined_small = lax.all_gather(small, "tensor", axis=0, tiled=True)
    products = [
        pltpu.VMEM((2 * each * devices, feat), F32),
        pltpu.VMEM((2 * each * devices, feat), F32),
        pltpu.VMEM((2 * each * devices, LANES), F32),
    ]
    back_small = pl.pallas_call(
        functools.partial(down_small_kernel, devices),
        out_shape=jax.ShapeDtypeStruct((experts * SMALL, LANES), BF16),
        in_specs=[anywhere, whole, anywhere],
        scratch_shapes=[
            pltpu.VMEM((experts * SMALL, LANES), F32),
            pltpu.VMEM(joined_small.shape, BF16),
            pltpu.VMEM(down.shape, BF16),
        ]
        + products
        + [pltpu.SemaphoreType.DMA((2 * len(chunks(hidden, 1024)),))],
        compiler_params=params(20),
    )(in_hbm(joined_small), up, in_hbm(down))
    back = pl.pallas_call(
        functools.partial(down_large_kernel, devices),
        out_shape=packed,
        in_specs=[anywhere, whole, anywhere, whole],
        scratch_shapes=[
            pltpu.VMEM((experts * BLOCK, LANES), F32),
            pltpu.VMEM((experts * SMALL, LANES), F32),
            pltpu.VMEM(joined.shape, BF16),
            pltpu.VMEM(down.shape, BF16),
        ]
        + products
        + [pltpu.SemaphoreType.DMA((3 * len(chunks(hidden, 1024)) + 1,))],
        compiler_params=params(20),
    )(in_hbm(joined), up, in_hbm(down), back_small)
    mixed, input_grad, prob_grad = pl.pallas_call(
        combine_kernel,
        out_shape=(
            jax.ShapeDtypeStruct((feat, count), BF16),
            jax.ShapeDtypeStruct((feat, count), BF16),
            jax.ShapeDtypeStruct((2, count), F32),
        ),
        scratch_shapes=stage,
        compiler_params=params(14),
    )(ids, probs, exchange(back, experts))
    return mixed.T, input_grad.T, prob_grad.T


def solution(mesh):
    return jax.shard_map(
        per_device,
        mesh=mesh,
        in_specs=(
            P("dp", "tensor"),
            P("dp", "tensor"),
            P("dp", None),
            P("dp", None),
            P("dp", "tensor", None),
            P("dp", None, "tensor"),
        ),
        out_specs=(P("dp", "tensor"), P("dp", "tensor"), P("dp", None)),
        check_vma=False,
    )
```

```python
import functools

import jax
import jax.numpy as jnp
from jax import lax
from jax.experimental import pallas as pl
from jax.experimental.pallas import tpu as pltpu
from jax.sharding import PartitionSpec as P

CAP = 3
LANES = 128
BLOCK = 24
SHARE = 40
HEAD = 16
SMALL = 8
LARGE = 16
F32 = jnp.float32
BF16 = jnp.bfloat16
MIB = 1024 * 1024


def params(mib):
    return pltpu.CompilerParams(vmem_limit_bytes=mib * MIB)


def one_hots(ids_ref, experts):
    tokens = ids_ref.shape[1]
    expert = lax.broadcasted_iota(jnp.int32, (experts, tokens), 0)
    named = [(ids_ref[k : k + 1, :] == expert).astype(F32) for k in range(2)]
    before = lax.broadcasted_iota(jnp.int32, (tokens, tokens), 0)
    after = lax.broadcasted_iota(jnp.int32, (tokens, tokens), 1)
    earlier = (before < after).astype(F32).astype(BF16)
    slot = jnp.dot((named[0] + named[1]).astype(BF16), earlier, preferred_element_type=F32)
    return named, slot


def tile_of(first, second, j):
    if j < 3:
        return first[:, j * LANES : (j + 1) * LANES]
    if j < 6:
        return second[:, (j - 3) * LANES : (j - 2) * LANES]
    return jnp.concatenate([first[:, 3 * LANES :], second[:, 3 * LANES :]], axis=1)


def pair_of(tiles):
    half = LANES // 2
    first = jnp.concatenate(tiles[0:3] + [tiles[6][:, :half]], axis=1)
    second = jnp.concatenate(tiles[3:6] + [tiles[6][:, half:]], axis=1)
    return first, second


def chunks(size, step):
    return [(at, min(at + step, size)) for at in range(0, size, step)]


def copies(sources, targets, semaphores):
    started = [
        pltpu.make_async_copy(source, target, semaphores.at[i])
        for i, (source, target) in enumerate(zip(sources, targets))
    ]
    for copy in started:
        copy.start()
    return started


def dispatch_kernel(
    ids_hbm,
    probs_hbm,
    tok_hbm,
    cot_hbm,
    _up,
    _down,
    out_ref,
    scratch,
    ids_ref,
    probs_ref,
    tok_ref,
    cot_ref,
    semaphores,
):
    experts = out_ref.shape[0] // BLOCK
    started = copies(
        (ids_hbm, probs_hbm, tok_hbm, cot_hbm),
        (ids_ref, probs_ref, tok_ref, cot_ref),
        semaphores,
    )
    for copy in started:
        copy.wait()
    named, slot = one_hots(ids_ref, experts)
    either = named[0] + named[1]
    weight = named[0] * probs_ref[0:1, :] + named[1] * probs_ref[1:2, :]
    across = (((1,), (1,)), ((), ()))
    for s in range(CAP):
        here = (slot == s).astype(F32)
        pick = (either * here).astype(BF16)
        rows = lax.dot_general(pick, tok_ref[...], across, preferred_element_type=F32)
        grads = lax.dot_general(pick, cot_ref[...], across, preferred_element_type=F32)
        grads = grads * jnp.sum(weight * here, axis=1, keepdims=True)
        for j in range(7):
            scratch[pl.ds(s * 7 + j, experts, stride=BLOCK), :] = tile_of(rows, grads, j)
    for r in range(7 * CAP, BLOCK):
        scratch[pl.ds(r, experts, stride=BLOCK), :] = jnp.zeros((experts, LANES), F32)
    out_ref[...] = scratch[...].astype(BF16)


def row_of(device, slot, each):
    return device * SHARE + (HEAD + (slot - 1) * each if slot else 0)


def up_kernel(
    block_ref, up_ref, down_ref, out_hbm, scratch, row_ref, grad_ref, out_ref, semaphores
):
    sources = block_ref.shape[0] // BLOCK
    feat, hidden = up_ref.shape
    devices = out_ref.shape[0] // SHARE
    each = sources // devices
    scratch[...] = block_ref[...].astype(F32)
    for d in range(devices):
        for s in range(CAP):
            rows = slice(row_of(d, s, each), row_of(d, s, each) + each)
            for j in range(7):
                tile = scratch[pl.ds(d * each * BLOCK + s * 7 + j, each, stride=BLOCK), :]
                if j < 3:
                    row_ref[rows, j * LANES : (j + 1) * LANES] = tile
                elif j < 6:
                    grad_ref[rows, (j - 3) * LANES : (j - 2) * LANES] = tile
                else:
                    row_ref[rows, 3 * LANES :] = tile
        pad = slice(d * SHARE + each, d * SHARE + HEAD)
        row_ref[pad, :] = jnp.zeros((HEAD - each, row_ref.shape[1]), F32)
        grad_ref[pad, :] = jnp.zeros((HEAD - each, grad_ref.shape[1]), F32)
    rows = row_ref[:, :feat].astype(BF16)
    grads = jnp.concatenate([grad_ref[...], row_ref[:, feat:]], axis=1).astype(BF16)
    started = []
    for left, weight, base in ((rows, up_ref, 0), (grads, down_ref, hidden)):
        for at, to in chunks(hidden, 512):
            span = slice(base + at, base + to)
            out_ref[:, span] = jnp.dot(
                left, weight[:, at:to], preferred_element_type=F32
            ).astype(BF16)
            started.append(
                pltpu.make_async_copy(
                    out_ref.at[:, span], out_hbm.at[:, span], semaphores.at[len(started)]
                )
            )
            started[-1].start()
    for copy in started:
        copy.wait()


def middle_kernel(sum_ref, small_ref, large_ref, scratch):
    hidden = sum_ref.shape[1] // 2
    each = small_ref.shape[0] // 2
    up_sum = sum_ref[:, :hidden].astype(F32)
    grad = sum_ref[:, hidden:].astype(F32)
    sigmoid = 1.0 / (1.0 + jnp.exp(-up_sum))
    act = (up_sum * sigmoid).astype(BF16).astype(F32)
    up_grad = grad * sigmoid * (1.0 + up_sum * (1.0 - sigmoid))
    score = jnp.sum(act * grad, axis=1, keepdims=True)
    high = score.astype(BF16).astype(F32)
    lane = lax.broadcasted_iota(jnp.int32, (sum_ref.shape[0], LANES), 1)
    score = jnp.where(lane == 0, high, jnp.where(lane == 1, score - high, 0.0))
    scratch[:each, :hidden] = act[:each]
    scratch[each:, :hidden] = up_grad[:each]
    scratch[:each, hidden:] = score[:each]
    scratch[each:, hidden:] = jnp.zeros((each, LANES), F32)
    small_ref[...] = scratch[...].astype(BF16)
    rest = slice(HEAD, HEAD + 2 * each)
    large_ref[:, :hidden] = act[rest].astype(BF16)
    large_ref[:, hidden : 2 * hidden] = up_grad[rest].astype(BF16)
    large_ref[:, 2 * hidden :] = score[rest].astype(BF16)


def columns_at(at, to):
    return (slice(None), slice(at, to))


def pack(out_ref, part_ref, scores, target, rows, devices, each, slots, height):
    for d in range(devices):
        for s in range(slots):
            low, high = rows(d, s)
            left = slice(low, low + each)
            right = slice(high, high + each)
            out, part = out_ref[left, :], part_ref[right, :]
            for j in range(7):
                target[pl.ds(d * each * height + s * 7 + j, each, stride=height), :] = tile_of(
                    out, part, j
                )
            target[pl.ds(d * each * height + 7 * slots + s, each, stride=height), :] = scores[
                left, :
            ]


def down_small_kernel(
    devices,
    join_hbm,
    up_ref,
    down_hbm,
    out_ref,
    target,
    join_ref,
    down_ref,
    out_rows,
    part_rows,
    score_rows,
    semaphores,
):
    hidden = up_ref.shape[1]
    across = (((1,), (1,)), ((), ()))
    spans = chunks(hidden, 1024)
    own = [columns_at(at, to) for at, to in spans]
    parts = own[:-1] + [columns_at(spans[-1][0], hidden + LANES)]
    count = len(spans)
    from_join = copies(
        [join_hbm.at[part] for part in parts], [join_ref.at[part] for part in parts], semaphores
    )
    from_down = copies(
        [down_hbm.at[part] for part in own],
        [down_ref.at[part] for part in own],
        semaphores.at[pl.ds(count, count)],
    )
    total = 0.0
    for i in range(count):
        from_join[i].wait()
        total += lax.dot_general(
            join_ref[own[i]], up_ref[own[i]], across, preferred_element_type=F32
        )
    part_rows[...] = total
    score_rows[...] = join_ref[:, hidden:].astype(F32)
    total = 0.0
    for i in range(count):
        from_down[i].wait()
        total += lax.dot_general(
            join_ref[own[i]], down_ref[own[i]], across, preferred_element_type=F32
        )
    out_rows[...] = total
    each = join_ref.shape[0] // devices // 2
    pack(
        out_rows,
        part_rows,
        score_rows,
        target,
        lambda d, s: (2 * each * d, 2 * each * d + each),
        devices,
        each,
        1,
        SMALL,
    )
    out_ref[...] = target[...].astype(BF16)


def down_large_kernel(
    devices,
    join_hbm,
    up_ref,
    down_hbm,
    out_ref,
    target,
    join_ref,
    down_ref,
    out_rows,
    part_rows,
    score_rows,
    semaphores,
):
    hidden = up_ref.shape[1]
    across = (((1,), (1,)), ((), ()))
    spans = chunks(hidden, 1024)
    parts = [columns_at(base + at, base + to) for base in (hidden, 0) for at, to in spans]
    parts.append(columns_at(2 * hidden, 2 * hidden + LANES))
    own = [columns_at(at, to) for at, to in spans]
    count = len(spans)
    from_join = copies(
        [join_hbm.at[part] for part in parts[:count]],
        [join_ref.at[part] for part in parts[:count]],
        semaphores,
    )
    from_down = copies(
        [down_hbm.at[part] for part in own],
        [down_ref.at[part] for part in own],
        semaphores.at[pl.ds(count, count)],
    )
    started = copies(
        [join_hbm.at[part] for part in parts[count:]],
        [join_ref.at[part] for part in parts[count:]],
        semaphores.at[pl.ds(2 * count, count + 1)],
    )
    total = 0.0
    for i in range(count):
        from_join[i].wait()
        total += lax.dot_general(
            join_ref[parts[i]], up_ref[own[i]], across, preferred_element_type=F32
        )
    part_rows[...] = total
    total = 0.0
    for i in range(count):
        from_down[i].wait()
        started[i].wait()
        total += lax.dot_general(
            join_ref[parts[count + i]], down_ref[own[i]], across, preferred_element_type=F32
        )
    out_rows[...] = total
    started[-1].wait()
    score_rows[...] = join_ref[parts[-1]].astype(F32)
    each = join_ref.shape[0] // devices // 2

    def rows(d, s):
        return ((2 * d + s) * each,) * 2

    pack(
        out_rows, part_rows, score_rows, target, rows, devices, each, 2, LARGE
    )
    out_ref[...] = target[...].astype(BF16)


def combine_kernel(
    ids_ref, probs_ref, small_ref, large_ref, mixed_ref, grad_ref, score_ref, first_rows, rest_rows
):
    experts = small_ref.shape[0] // SMALL
    named, slot = one_hots(ids_ref, experts)
    first_rows[...] = small_ref[...].astype(F32)
    rest_rows[...] = large_ref[...].astype(F32)

    def came(slot, j):
        if slot == 0:
            return first_rows[pl.ds(j, experts, stride=SMALL), :]
        at = (slot - 1) * 7 + j if j < 7 else 14 + slot - 1
        return rest_rows[pl.ds(at, experts, stride=LARGE), :]

    along = (((0,), (0,)), ((), ()))
    outs, parts, picks = [], [], []
    scores = [jnp.zeros((1, ids_ref.shape[1]), F32) for _ in range(2)]
    for s in range(CAP):
        here = (slot == s).astype(F32)
        first, second = pair_of([came(s, j) for j in range(7)])
        outs.append(first)
        parts.append(second)
        picks.append(jnp.concatenate([named[0] * here, named[1] * here], axis=1))
        tail = came(s, 7)
        value = tail[:, 0:1] + tail[:, 1:2]
        for k in range(2):
            scores[k] += jnp.sum(named[k] * here * value, axis=0, keepdims=True)
    outs = jnp.concatenate(outs, axis=0).astype(BF16)
    parts = jnp.concatenate(parts, axis=0).astype(BF16)
    picks = jnp.concatenate(picks, axis=0)
    tokens = ids_ref.shape[1]
    either = (picks[:, :tokens] + picks[:, tokens:]).astype(BF16)
    got = lax.dot_general(outs, picks.astype(BF16), along, preferred_element_type=F32)
    mixed_ref[...] = (
        got[:, :tokens] * probs_ref[0:1, :] + got[:, tokens:] * probs_ref[1:2, :]
    ).astype(BF16)
    grad_ref[...] = lax.dot_general(parts, either, along, preferred_element_type=F32).astype(BF16)
    score_ref[...] = jnp.concatenate(scores, axis=0) / probs_ref[...]


def gather_by_pairs(rows, devices):
    pairs = [[i, i + 1] for i in range(0, devices, 2)]
    parities = [list(range(i, devices, 2)) for i in range(2)]
    for groups in (pairs, parities):
        rows = lax.all_gather(rows, "tensor", axis=0, tiled=True, axis_index_groups=groups)
    return rows


def in_vmem(array):
    return pltpu.with_memory_space_constraint(array, pltpu.VMEM)


def in_hbm(array):
    return pltpu.with_memory_space_constraint(array, pltpu.HBM)


def exchange(block, experts):
    shape = block.shape
    block = block.reshape(experts, -1, LANES)
    block = lax.all_to_all(block, "dp", split_axis=0, concat_axis=0, tiled=True)
    return block.reshape(shape)


def per_device(tokens, cotangent, expert_ids, route_probs, up_weight, down_weight):
    count, feat = tokens.shape
    experts = lax.axis_size("dp")
    hidden = up_weight.shape[2]
    ids, probs = expert_ids.T, route_probs.T
    up, down = up_weight[0], down_weight[0].T
    packed = jax.ShapeDtypeStruct((experts * BLOCK, LANES), BF16)
    stage = [pltpu.VMEM((experts * BLOCK, LANES), F32)]
    anywhere = pl.BlockSpec(memory_space=pltpu.HBM)
    send = pl.pallas_call(
        dispatch_kernel,
        out_shape=packed,
        in_specs=[anywhere] * 6,
        scratch_shapes=stage
        + [
            pltpu.VMEM(ids.shape, jnp.int32),
            pltpu.VMEM(probs.shape, F32),
            pltpu.VMEM((feat, count), BF16),
            pltpu.VMEM((feat, count), BF16),
            pltpu.SemaphoreType.DMA((4,)),
        ],
        compiler_params=params(14),
    )(*map(in_hbm, (ids, probs, tokens.T, cotangent.T, up, down)))
    devices = lax.axis_size("tensor")
    each = experts // devices
    partial = pl.pallas_call(
        up_kernel,
        out_shape=pltpu.HBM((devices * SHARE, 2 * hidden), BF16),
        out_specs=anywhere,
        scratch_shapes=stage
        + [
            pltpu.VMEM((devices * SHARE, 4 * LANES), F32),
            pltpu.VMEM((devices * SHARE, 3 * LANES), F32),
            pltpu.VMEM((devices * SHARE, 2 * hidden), BF16),
            pltpu.SemaphoreType.DMA((2 * len(chunks(hidden, 512)),)),
        ],
        compiler_params=params(20),
    )(exchange(send, experts), in_vmem(up), in_vmem(down))
    share = lax.psum_scatter(partial, "tensor", scatter_dimension=0, tiled=True)
    small, large = pl.pallas_call(
        middle_kernel,
        out_shape=(
            jax.ShapeDtypeStruct((2 * each, hidden + LANES), BF16),
            jax.ShapeDtypeStruct((2 * each, 2 * hidden + LANES), BF16),
        ),
        scratch_shapes=[pltpu.VMEM((2 * each, hidden + LANES), F32)],
        compiler_params=params(14),
    )(share)
    whole = pl.BlockSpec(memory_space=pltpu.VMEM)
    joined = lax.all_gather(large, "tensor", axis=0, tiled=True)
    joined_small = gather_by_pairs(small, devices)
    products = [
        pltpu.VMEM((2 * each * devices, feat), F32),
        pltpu.VMEM((2 * each * devices, feat), F32),
        pltpu.VMEM((2 * each * devices, LANES), F32),
    ]
    back_small = pl.pallas_call(
        functools.partial(down_small_kernel, devices),
        out_shape=jax.ShapeDtypeStruct((experts * SMALL, LANES), BF16),
        in_specs=[anywhere, whole, anywhere],
        scratch_shapes=[
            pltpu.VMEM((experts * SMALL, LANES), F32),
            pltpu.VMEM(joined_small.shape, BF16),
            pltpu.VMEM(down.shape, BF16),
        ]
        + products
        + [pltpu.SemaphoreType.DMA((2 * len(chunks(hidden, 1024)),))],
        compiler_params=params(20),
    )(in_hbm(joined_small), up, in_hbm(down))
    back_small = exchange(back_small, experts)
    back = pl.pallas_call(
        functools.partial(down_large_kernel, devices),
        out_shape=jax.ShapeDtypeStruct((experts * LARGE, LANES), BF16),
        in_specs=[anywhere, whole, anywhere],
        scratch_shapes=[
            pltpu.VMEM((experts * LARGE, LANES), F32),
            pltpu.VMEM(joined.shape, BF16),
            pltpu.VMEM(down.shape, BF16),
        ]
        + products
        + [pltpu.SemaphoreType.DMA((3 * len(chunks(hidden, 1024)) + 1,))],
        compiler_params=params(20),
    )(in_hbm(joined), up, in_hbm(down))
    mixed, input_grad, prob_grad = pl.pallas_call(
        combine_kernel,
        out_shape=(
            jax.ShapeDtypeStruct((feat, count), BF16),
            jax.ShapeDtypeStruct((feat, count), BF16),
            jax.ShapeDtypeStruct((2, count), F32),
        ),
        scratch_shapes=[
            pltpu.VMEM((experts * SMALL, LANES), F32),
            pltpu.VMEM((experts * LARGE, LANES), F32),
        ],
        compiler_params=params(14),
    )(ids, probs, back_small, exchange(back, experts))
    return mixed.T, input_grad.T, prob_grad.T


def solution(mesh):
    return jax.shard_map(
        per_device,
        mesh=mesh,
        in_specs=(
            P("dp", "tensor"),
            P("dp", "tensor"),
            P("dp", None),
            P("dp", None),
            P("dp", "tensor", None),
            P("dp", None, "tensor"),
        ),
        out_specs=(P("dp", "tensor"), P("dp", "tensor"), P("dp", None)),
        check_vma=False,
    )
```
